128 devices in a mesh: fsdp: 16 (over y, x), batch: 8 (over z, core).
Axes of the slice: x: 4, y: 4, z: 4, core: 2. Of those that a mesh axis runs over, the one named last changes fastest.
Arguments:
- inputs: float32 [32768, 1024], P(('fsdp', 'batch')), may hold values from -6 to 6
- cotangent: float32 [32768, 1024], P(('fsdp', 'batch'))
- segment_ids: int32 [32768], P(('fsdp', 'batch')), may hold values from 0 to 4, as said below
- routed: int32 [16, 256], P('fsdp'), may hold values from 0 to 2047, as said below
- qkv_master: float32 [2, 1024, 3072], P(None, ('fsdp', 'batch')), may hold values from -0.1875 to 0.1875
- out_master: float32 [2, 1024, 1024], P(None, ('fsdp', 'batch')), may hold values from -3 to 3
- up_master: float32 [2, 4096, 1024], P(None, ('fsdp', 'batch')), may hold values from -0.1875 to 0.1875
- down_master: float32 [2, 4096, 1024], P(None, ('fsdp', 'batch')), may hold values from -0.09375 to 0.09375
- qkv_moment: float32 [2, 1024, 3072], P(None, ('fsdp', 'batch'))
- out_moment: float32 [2, 1024, 1024], P(None, ('fsdp', 'batch'))
- up_moment: float32 [2, 4096, 1024], P(None, ('fsdp', 'batch'))
- down_moment: float32 [2, 4096, 1024], P(None, ('fsdp', 'batch'))
- router: float32 [1024], replicated, may hold values from -0.1875 to 0.1875
- router_first: float32 [1024], replicated, may hold values from -2560 to 2560
- router_second: float32 [1024], replicated, may hold values from 880803.8 to 3523215.2
Outputs:
- mixed: float32 [32768, 1024], P(('fsdp', 'batch'))
- grad_inputs: float32 [32768, 1024], P(('fsdp', 'batch'))
- new_qkv_moment: float32 [2, 1024, 3072], P(None, ('fsdp', 'batch'))
- new_out_moment: float32 [2, 1024, 1024], P(None, ('fsdp', 'batch'))
- new_up_moment: float32 [2, 4096, 1024], P(None, ('fsdp', 'batch'))
- new_down_moment: float32 [2, 4096, 1024], P(None, ('fsdp', 'batch'))
- new_qkv_master: float32 [2, 1024, 3072], P(None, ('fsdp', 'batch'))
- new_out_master: float32 [2, 1024, 1024], P(None, ('fsdp', 'batch'))
- new_up_master: float32 [2, 4096, 1024], P(None, ('fsdp', 'batch'))
- new_down_master: float32 [2, 4096, 1024], P(None, ('fsdp', 'batch'))
- qkv_copy: bfloat16 [2, 1024, 3072], P(None, ('fsdp', 'batch'))
- out_copy: bfloat16 [2, 1024, 1024], P(None, ('fsdp', 'batch'))
- up_copy: bfloat16 [2, 4096, 1024], P(None, ('fsdp', 'batch'))
- down_copy: bfloat16 [2, 4096, 1024], P(None, ('fsdp', 'batch'))
- new_router: float32 [1024], replicated
- new_router_first: float32 [1024], replicated
- new_router_second: float32 [1024], replicated
The draws below stay inside these ranges and needn't reach their ends.
Inputs may be any that keep to these rules, and one draw needn't show every extreme that they name: `segment_ids`: within each sequence of 2048 positions the numbers never fall, and one segment covers positions 128 to 1919. `routed`: each row holds 256 distinct positions of its sequence in rising order, among them 0 and 2047.
All inputs are finite; a program needn't handle non-finite values.
Results may differ from the reference program's by a relative error of at most 0.017.
The reference program's roundings to bfloat16 on the way count: a program that leaves them out, or rounds other values in their place, can miss the bound.
Values may be sent and summed in bfloat16 or wider, within the bound.
No kernel may reach another device: no remote copies, remote signals or barrier semaphores. Data moves between devices by JAX's collectives and lax.ppermute only.
A program may use at most 384 MiB of HBM per device.

```python
import math
import jax
import jax.numpy as jnp
from jax import lax

D = 1024
HEADS = 16
HDIM = 64
FF = 4096
TOK_DEV = 256
LAYERS = 2
NS_ITERS = 2
STEP = 8
SEQS = 16
SEQ_LEN = 2048
K_ROUTE = 256
TOKENS = 32768


def draw_cotangent(key, part):
    key = jax.random.fold_in(key, 11)
    row_index = jnp.arange(TOKENS)
    sequence_of = (row_index // SEQ_LEN).astype(jnp.float32)
    position = (row_index % SEQ_LEN).astype(jnp.float32)
    base_noise = jax.random.normal(key, (TOKENS, D), jnp.float32)
    factor = (1.0 + 2.0 * sequence_of / SEQS) * (1.0 + 2.0 * position / SEQ_LEN) / 2.0
    return base_noise * factor[:, None]


def draw_segment_ids(key, part):
    key = jax.random.fold_in(key, 3)
    sub_keys = jax.random.split(key, 4)
    half_dev = TOK_DEV // 2
    head_len = jax.random.randint(sub_keys[0], (SEQS, 1), 1, half_dev + 1)
    tail_len = jax.random.randint(sub_keys[1], (SEQS, 1), 2, half_dev + 1)
    early_cut = jnp.minimum(jax.random.randint(sub_keys[2], (SEQS, 1), 1, half_dev + 1), head_len)
    late_cut = jnp.maximum(SEQ_LEN - jax.random.randint(sub_keys[3], (SEQS, 1), 1, half_dev), SEQ_LEN - tail_len + 1)
    position = jnp.arange(SEQ_LEN)[None, :]
    numbers = (position >= early_cut).astype(jnp.int32) + (position >= head_len).astype(jnp.int32)
    numbers = numbers + (position >= SEQ_LEN - tail_len).astype(jnp.int32) + (position >= late_cut).astype(jnp.int32)
    return numbers.reshape(TOKENS).astype(jnp.int32)


def draw_routed(key, part):
    key = jax.random.fold_in(key, 5)
    shard_count = SEQ_LEN // TOK_DEV
    slot_share = K_ROUTE // shard_count
    leading = shard_count // 2 - 1
    trailing = K_ROUTE - leading * slot_share

    def one_sequence(seq_index):
        seq_key = jax.random.fold_in(key, seq_index)
        pieces = []
        for block_index in range(leading):
            offsets = jnp.sort(jax.random.permutation(jax.random.fold_in(seq_key, block_index), TOK_DEV)[:slot_share])
            pieces.append((offsets + (block_index + shard_count // 2) * TOK_DEV).astype(jnp.int32))
        tail_offsets = jnp.sort(jax.random.permutation(jax.random.fold_in(seq_key, 97), TOK_DEV - 1)[:trailing - 1])
        pieces.append((tail_offsets + (shard_count - 1) * TOK_DEV).astype(jnp.int32))
        pieces.append(jnp.full((1,), SEQ_LEN - 1, jnp.int32))
        joined = jnp.concatenate(pieces).astype(jnp.int32)
        return joined.at[0].set(0)
    return jax.vmap(one_sequence)(jnp.arange(SEQS)).astype(jnp.int32)


def moment_layers(key, base_noise, base_scale, row_count, col_count):
    column = jnp.exp(jax.random.uniform(jax.random.fold_in(key, 7), (LAYERS, 1, col_count), jnp.float32, 0.0, 1.386))
    row_scale = 10.0 ** (jnp.arange(row_count, dtype=jnp.float32) / row_count)
    layer_scale = jnp.where(jnp.arange(LAYERS) == 0, base_scale * TOKENS ** 0.5, base_scale * (SEQS * K_ROUTE) ** 0.5).astype(jnp.float32)
    return base_noise * column * row_scale[None, :, None] * layer_scale[:, None, None]


def draw_qkv_moment(key, part):
    key = jax.random.fold_in(key, 21)
    base_noise = jax.random.normal(key, (LAYERS, D, 3 * D), jnp.float32)
    return moment_layers(key, base_noise, 0.08, D, 3 * D)


def draw_out_moment(key, part):
    key = jax.random.fold_in(key, 22)
    base_noise = jax.random.normal(key, (LAYERS, D, D), jnp.float32)
    return moment_layers(key, base_noise, 0.01, D, D)


def draw_up_moment(key, part):
    key = jax.random.fold_in(key, 23)
    base_noise = jax.random.normal(key, (LAYERS, FF, D), jnp.float32)
    return moment_layers(key, base_noise, 0.08, FF, D)


def draw_down_moment(key, part):
    key = jax.random.fold_in(key, 24)
    base_noise = jax.random.normal(key, (LAYERS, FF, D), jnp.float32)
    return moment_layers(key, base_noise, 0.08, FF, D)


def shard_levels(key, dims, shards, least, top_value):
    level = 1.0
    for axis_at, shards_of in shards:
        heights = jax.random.uniform(jax.random.fold_in(jax.random.fold_in(key, 6), axis_at), (shards_of,), jnp.float32, least / len(shards), top_value / len(shards))
        level = level * jnp.repeat(jnp.exp(heights), dims[axis_at] // shards_of).reshape((-1,) + (1,) * (len(dims) - 1 - axis_at))
    return level


def gaussian(own_key, dims, deviation, limit, cuts=(), kind=jnp.bfloat16):
    drawn = jax.random.normal(own_key, dims, jnp.float32) * deviation
    if len(cuts) > 0:
        drawn = shard_levels(own_key, dims, cuts, -0.22, 0.18) * drawn
    return jnp.clip(drawn, min=-limit, max=limit).astype(kind)


def setup_inputs(seed: int = 0) -> dict:
    keys = jax.random.split(jax.random.key(seed), 16)
    return {
        "inputs": gaussian(keys[0], (TOKENS, D), 1.0, 6.0, ((0, 128),), jnp.float32),
        "cotangent": draw_cotangent(jax.random.fold_in(keys[15], 71), 0),
        "segment_ids": draw_segment_ids(jax.random.fold_in(keys[15], 71), 0),
        "routed": draw_routed(jax.random.fold_in(keys[15], 71), 0),
        "qkv_master": gaussian(keys[4], (LAYERS, D, 3 * D), D ** -0.5, 0.1875, ((1, 128),), jnp.float32),
        "out_master": gaussian(keys[5], (LAYERS, D, D), (8 * D // SEQ_LEN) ** -0.5, 3.0, ((1, 128),), jnp.float32),
        "up_master": gaussian(keys[6], (LAYERS, FF, D), D ** -0.5, 0.1875, ((1, 128),), jnp.float32),
        "down_master": gaussian(keys[7], (LAYERS, FF, D), FF ** -0.5, 0.09375, ((1, 128),), jnp.float32),
        "qkv_moment": draw_qkv_moment(jax.random.fold_in(keys[15], 71), 0),
        "out_moment": draw_out_moment(jax.random.fold_in(keys[15], 71), 0),
        "up_moment": draw_up_moment(jax.random.fold_in(keys[15], 71), 0),
        "down_moment": draw_down_moment(jax.random.fold_in(keys[15], 71), 0),
        "router": gaussian(keys[12], (D,), D ** -0.5, 0.1875, (), jnp.float32),
        "router_first": gaussian(keys[13], (D,), (0.22 * (D * SEQS * K_ROUTE) ** 0.5), 2560.0, (), jnp.float32),
        "router_second": jnp.clip(jnp.exp(jax.random.uniform(keys[14], (D,), jnp.float32, math.log(880803.8), math.log(3523215.2))), 880803.8, 3523215.2),
    }


EPSILON = 1e-05
SCORE_SCALE = 0.125
NEGATIVE = -1e+30
MOMENTUM = 0.95
WEIGHT_DECAY = 0.01
STEP_RATES = (0.15, 1.0, 0.15, 0.15)
NEWTON_A = 3.4445
NEWTON_B = -4.775
NEWTON_C = 2.0315
NEWTON_EPSILON = 1e-07
ADAM_RATE = 0.03
FIRST_DECAY = 0.9
SECOND_DECAY = 0.95
ADAM_EPSILON = 1e-08
HIGHEST = lax.Precision.HIGHEST

@jax.custom_vjp
def low(v):
    return lax.optimization_barrier(v.astype(jnp.bfloat16)).astype(jnp.float32)

@jax.custom_vjp
def low_back(v):
    return v

def low_keep(v):
    return (low(v), None)

def low_pass(kept, grad):
    return (grad,)

def back_keep(v):
    return (v, None)

def back_low(kept, grad):
    return (low(grad),)
low.defvjp(low_keep, low_pass)
low_back.defvjp(back_keep, back_low)

def rms_norm(values):
    return values * lax.rsqrt(lax.optimization_barrier(jnp.mean(values * values, axis=-1, keepdims=True)) + EPSILON)

def matmul(left, right):
    return jnp.dot(left, right, precision=HIGHEST)

def attention(normed, weight_qkv, weight_out, segment):
    row_count = normed.shape[0]
    projected = low(low_back(matmul(normed, weight_qkv)))
    queries = projected[:, :D].reshape(row_count, HEADS, HDIM)
    keys_all = projected[:, D:2 * D].reshape(row_count, HEADS, HDIM)
    values_all = projected[:, 2 * D:].reshape(row_count, HEADS, HDIM)
    block_width = min(512, row_count)
    key_pos = jnp.arange(row_count)

    def score_block(first_row):
        query_block = lax.dynamic_slice_in_dim(queries, first_row, block_width, 0)
        query_pos = first_row + jnp.arange(block_width)
        query_seg = lax.dynamic_slice_in_dim(segment, first_row, block_width, 0)
        scores = low_back(jnp.einsum('qhd,khd->hqk', query_block, keys_all, precision=HIGHEST) * SCORE_SCALE)
        allowed = (key_pos[None, :] <= query_pos[:, None]) & (segment[None, :] == query_seg[:, None])
        scores = jnp.where(allowed[None], scores, NEGATIVE)
        row_top = lax.optimization_barrier(jnp.max(scores, axis=-1, keepdims=True))
        exponent = jnp.exp(scores - row_top)
        attention_probs = low(exponent / lax.optimization_barrier(jnp.sum(exponent, axis=-1, keepdims=True)))
        return jnp.einsum('hqk,khd->qhd', attention_probs, values_all, precision=HIGHEST).reshape(block_width, D)
    first_rows = (jnp.arange(row_count // block_width) * block_width).astype(jnp.int32)
    mixed_heads = lax.map(jax.checkpoint(score_block), first_rows).reshape(row_count, D)
    mixed_heads = low(low_back(mixed_heads))
    return low_back(jnp.dot(mixed_heads, weight_out.T, precision=HIGHEST))

def feed_forward(normed, weight_up, weight_down):
    hidden = low_back(jnp.dot(normed, weight_up.T, precision=HIGHEST))
    active = low(jax.nn.gelu(hidden, approximate=True))
    return low_back(matmul(active, weight_down))

def layer_block(inputs, normed, weights, segment):
    attended = attention(low(normed), weights[0], weights[1], segment)
    middle = inputs + attended
    fed_branch = feed_forward(low(rms_norm(middle)), weights[2], weights[3])
    return (attended, middle, fed_branch)

def forward(weights, values, segment, chosen):
    dense_weights, routed_weights, router_vector = weights
    attended, middle, fed_branch = layer_block(values, rms_norm(values), dense_weights, segment)
    hidden = middle + fed_branch
    slot_rows = hidden[chosen]
    slot_normed = rms_norm(slot_rows)
    gate_values = jnp.dot(slot_normed, router_vector, precision=HIGHEST)
    routed_attended, routed_middle, routed_fed = layer_block(slot_rows, slot_normed, routed_weights, segment[chosen])
    return hidden.at[chosen].add(gate_values[:, None] * (routed_attended + routed_fed))

def orthogonalize(moment, block_width):
    row_count = moment.shape[0]
    grouped = moment.reshape(row_count, moment.shape[1] // block_width, block_width)
    for iteration in range(NS_ITERS):
        gram_sum = jnp.einsum('rgb,rgc->gbc', grouped, grouped, precision=HIGHEST)
        if iteration == 0:
            norm_scale = jnp.sqrt(jnp.trace(gram_sum, axis1=1, axis2=2)) + NEWTON_EPSILON
            grouped = grouped / norm_scale[None, :, None]
            gram_sum = gram_sum / (norm_scale * norm_scale)[:, None, None]
        product = jnp.einsum('rgb,gbc->rgc', grouped, gram_sum, precision=HIGHEST)
        grouped = NEWTON_A * grouped + NEWTON_B * product + NEWTON_C * jnp.einsum('rgb,gbc->rgc', product, gram_sum, precision=HIGHEST)
    return grouped.reshape(row_count, -1)

def reference(inputs, cotangent, segment_ids, routed, qkv_master, out_master, up_master, down_master, qkv_moment, out_moment, up_moment, down_moment, router, router_first, router_second):
    masters = (qkv_master, out_master, up_master, down_master)
    moments = (qkv_moment, out_moment, up_moment, down_moment)
    weight_copies = [matrix.astype(jnp.bfloat16).astype(jnp.float32) for matrix in masters]
    params = (tuple((weight_copy[0] for weight_copy in weight_copies)), tuple((weight_copy[1] for weight_copy in weight_copies)), router)
    sequences = (inputs.reshape(SEQS, SEQ_LEN, D), cotangent.reshape(SEQS, SEQ_LEN, D), segment_ids.reshape(SEQS, SEQ_LEN), routed)
    initial = jax.tree.map(jnp.zeros_like, params)

    def accumulate(running, sequence_item):
        seq_inputs, seq_cotangent, seq_segment, seq_routed = sequence_item
        result, pull_back = jax.vjp(lambda weights, values: forward(weights, values, seq_segment, seq_routed), params, seq_inputs)
        weight_grads, input_grads = pull_back(seq_cotangent)
        return (jax.tree.map(jnp.add, running, weight_grads), (result, input_grads))
    totals, (mixed, grad_inputs) = lax.scan(accumulate, initial, sequences)
    widths = (HDIM, HDIM, D, D)
    full_rows = (D, D, FF, FF)
    new_moments = []
    new_masters = []
    for index_type in range(4):
        gradient = jnp.stack([totals[0][index_type], totals[1][index_type]])
        moment_new = MOMENTUM * moments[index_type] + gradient
        ortho = jnp.stack([orthogonalize(moment_new[layer_index], widths[index_type]) for layer_index in range(LAYERS)])
        rate = STEP_RATES[index_type]
        factor = 0.2 * math.sqrt(max(full_rows[index_type], widths[index_type]))
        new_moments.append(moment_new)
        new_masters.append(masters[index_type] * (1.0 - rate * WEIGHT_DECAY) - rate * factor * ortho)
    router_grad = totals[2]
    first_new = FIRST_DECAY * router_first + (1.0 - FIRST_DECAY) * router_grad
    second_new = SECOND_DECAY * router_second + (1.0 - SECOND_DECAY) * router_grad * router_grad
    corrected_first = first_new / (1.0 - FIRST_DECAY ** STEP)
    corrected_second = second_new / (1.0 - SECOND_DECAY ** STEP)
    router_new = router * (1.0 - ADAM_RATE * WEIGHT_DECAY) - ADAM_RATE * corrected_first / (jnp.sqrt(corrected_second) + ADAM_EPSILON)
    return (mixed.reshape(TOKENS, D), grad_inputs.reshape(TOKENS, D), new_moments[0], new_moments[1], new_moments[2], new_moments[3], new_masters[0], new_masters[1], new_masters[2], new_masters[3], new_masters[0].astype(jnp.bfloat16), new_masters[1].astype(jnp.bfloat16), new_masters[2].astype(jnp.bfloat16), new_masters[3].astype(jnp.bfloat16), router_new, first_new, second_new)
```

```python
import math

import jax
import jax.numpy as jnp
from jax import lax
from jax.sharding import Mesh
from jax.sharding import PartitionSpec as P

D = 1024
HEADS = 16
HDIM = 64
FF = 4096
STEP = 8
N_FSDP = 16
N_BATCH = 8
LOCAL_HEADS = HEADS // N_BATCH
LOCAL_WIDTH = LOCAL_HEADS * HDIM
K_ROUTE = 256

EPSILON = 1e-05
SCORE_SCALE = 0.125
NEGATIVE = -1e30
MOMENTUM = 0.95
WEIGHT_DECAY = 0.01
STEP_RATES = (0.15, 1.0, 0.15, 0.15)
NEWTON_A = 3.4445
NEWTON_B = -4.775
NEWTON_C = 2.0315
NEWTON_EPSILON = 1e-07
ADAM_RATE = 0.03
FIRST_DECAY = 0.9
SECOND_DECAY = 0.95
ADAM_EPSILON = 1e-08
HIGHEST = lax.Precision.HIGHEST
HIGH = lax.Precision.HIGH
F32 = jnp.float32
BF16 = jnp.bfloat16

FSDP = ("y", "x")
BATCH = ("z", "c")
EVERY = ("y", "x", "z", "c")


def rms_norm(values):
    return values * lax.rsqrt(jnp.mean(values * values, axis=-1, keepdims=True) + EPSILON)


def gelu_tanh(values):
    return jax.nn.gelu(values, approximate=True)


def norm_back(values, grad_normed):
    pull_back = jax.vjp(rms_norm, values)[1]
    return pull_back(grad_normed)[0]


def dot_f32(pattern, left, right):
    return jnp.einsum(pattern, left, right, preferred_element_type=F32)


def gather_batch(values):
    return lax.all_gather(values, BATCH, axis=0, tiled=True)


def scatter_batch(values):
    return lax.psum_scatter(values, BATCH, scatter_dimension=0, tiled=True)


def head_shards(masters):
    joined = jnp.concatenate([masters[0].astype(BF16), masters[1].astype(BF16)], axis=2)
    parts = joined.reshape(2, 8, 4, N_BATCH, LOCAL_WIDTH)
    parts = jnp.transpose(parts, (3, 0, 1, 2, 4)).reshape(N_BATCH, 2, 8, 4 * LOCAL_WIDTH)
    moved = lax.all_to_all(parts, BATCH, split_axis=0, concat_axis=0, tiled=True)
    return jnp.transpose(moved, (1, 0, 2, 3)).reshape(2, 64, 4 * LOCAL_WIDTH)


def attend(projected, positions, segments):
    rows = projected.shape[0]
    queries = projected[:, :LOCAL_WIDTH].reshape(rows, LOCAL_HEADS, HDIM)
    keys = projected[:, LOCAL_WIDTH : 2 * LOCAL_WIDTH].reshape(rows, LOCAL_HEADS, HDIM)
    values = projected[:, 2 * LOCAL_WIDTH :].reshape(rows, LOCAL_HEADS, HDIM)
    allowed = (positions[None, :] <= positions[:, None]) & (segments[None, :] == segments[:, None])
    scores = dot_f32("qhd,khd->hqk", queries, keys) * SCORE_SCALE
    scores = jnp.where(allowed[None], scores, NEGATIVE)
    row_top = jnp.max(scores, axis=2, keepdims=True)
    exponent = jnp.exp(scores - row_top)
    row_total = jnp.sum(exponent, axis=2, keepdims=True)
    probs = (exponent / row_total).astype(BF16)
    mixed = dot_f32("hqk,khd->qhd", probs, values).reshape(rows, LOCAL_WIDTH).astype(BF16)
    return mixed, row_top + jnp.log(row_total)


def attend_back(projected, positions, segments, log_total, grad_mixed):
    rows = projected.shape[0]
    queries = projected[:, :LOCAL_WIDTH].reshape(rows, LOCAL_HEADS, HDIM)
    keys = projected[:, LOCAL_WIDTH : 2 * LOCAL_WIDTH].reshape(rows, LOCAL_HEADS, HDIM)
    values = projected[:, 2 * LOCAL_WIDTH :].reshape(rows, LOCAL_HEADS, HDIM)
    grads = grad_mixed.reshape(rows, LOCAL_HEADS, HDIM)
    allowed = (positions[None, :] <= positions[:, None]) & (segments[None, :] == segments[:, None])
    scores = dot_f32("qhd,khd->hqk", queries, keys) * SCORE_SCALE
    probs = jnp.exp(jnp.where(allowed[None], scores, NEGATIVE) - log_total)
    grad_probs = dot_f32("qhd,khd->hqk", grads, values)
    inner = jnp.sum(probs * grad_probs, axis=2, keepdims=True)
    grad_scores = (probs * (grad_probs - inner)).astype(BF16) * SCORE_SCALE
    grad_q = dot_f32("hqk,khd->qhd", grad_scores, keys).reshape(rows, LOCAL_WIDTH)
    grad_k = dot_f32("hqk,qhd->khd", grad_scores, queries).reshape(rows, LOCAL_WIDTH)
    grad_v = dot_f32("hqk,qhd->khd", probs.astype(BF16), grads).reshape(rows, LOCAL_WIDTH)
    return jnp.concatenate([grad_q, grad_k, grad_v], axis=1).astype(BF16)


def qkv_forward(normed_all, weight_heads):
    return dot_f32("td,dc->tc", normed_all, weight_heads[:, : 3 * LOCAL_WIDTH]).astype(BF16)


def out_forward(mixed, weight_heads):
    return dot_f32("td,od->to", mixed, weight_heads[:, 3 * LOCAL_WIDTH :])


def feed_forward(normed_all, weight_up, weight_down):
    hidden = dot_f32("td,fd->tf", normed_all, weight_up)
    active = gelu_tanh(hidden).astype(BF16)
    return dot_f32("tf,fd->td", active, weight_down), hidden, active


def feed_backward(normed_all, weight_up, weight_down, hidden, active, grad_low):
    grad_down = dot_f32("tf,td->fd", active, grad_low)
    grad_active = dot_f32("td,fd->tf", grad_low, weight_down)
    pull_back = jax.vjp(gelu_tanh, hidden)[1]
    grad_hidden = pull_back(grad_active)[0].astype(BF16)
    grad_up = dot_f32("tf,td->fd", grad_hidden, normed_all)
    grad_normed = dot_f32("tf,fd->td", grad_hidden, weight_up)
    return grad_normed, grad_up, grad_down


def attention_grads(normed_all, weight_heads, mixed, projected, positions, segments, log_total, grad_low):
    grad_out = dot_f32("to,td->od", grad_low, mixed)
    grad_mixed = dot_f32("to,od->td", grad_low, weight_heads[:, 3 * LOCAL_WIDTH :]).astype(BF16)
    grad_projected = attend_back(projected, positions, segments, log_total, grad_mixed)
    grad_qkv = dot_f32("td,tc->dc", normed_all, grad_projected)
    grad_normed = dot_f32("tc,dc->td", grad_projected, weight_heads[:, : 3 * LOCAL_WIDTH])
    return grad_normed, jnp.concatenate([grad_qkv, grad_out], axis=1)


def polynomial(rows, gram):
    once = jnp.einsum("rb,bc->rc", rows, gram, precision=HIGH)
    twice = jnp.einsum("rb,bc->rc", once, gram, precision=HIGH)
    return NEWTON_A * rows + NEWTON_B * once + NEWTON_C * twice


def newton_two(rows, gram):
    scale = jnp.sqrt(jnp.trace(gram)) + NEWTON_EPSILON
    rows = rows / scale
    gram = gram / (scale * scale)

    def second_gram(values):
        inner = polynomial(values, gram)
        return polynomial(jnp.einsum("rb,bc->rc", inner, gram, precision=HIGH), gram)

    first = polynomial(rows, gram)
    once = second_gram(first)
    twice = second_gram(once)
    return NEWTON_A * first + NEWTON_B * once + NEWTON_C * twice


def newton_heads(block):
    for iteration in range(2):
        gram = jnp.einsum("rb,rc->bc", block, block, precision=HIGHEST)
        if iteration == 0:
            scale = jnp.sqrt(jnp.trace(gram)) + NEWTON_EPSILON
            block = block / scale
            gram = gram / (scale * scale)
        product = jnp.einsum("rb,bc->rc", block, gram, precision=HIGHEST)
        block = (
            NEWTON_A * block
            + NEWTON_B * product
            + NEWTON_C * jnp.einsum("rb,bc->rc", product, gram, precision=HIGHEST)
        )
    return block


def body(
    inputs,
    cotangent,
    segment_ids,
    routed,
    qkv_master,
    out_master,
    up_master,
    down_master,
    qkv_moment,
    out_moment,
    up_moment,
    down_moment,
    router,
    router_first,
    router_second,
):
    masters = (qkv_master, out_master, up_master, down_master)
    token_count = inputs.shape[0]
    batch_index = lax.axis_index(BATCH)
    core_index = lax.axis_index("c")
    sequence_pos = jnp.arange(token_count * N_BATCH)
    slot_pos = jnp.arange(K_ROUTE)
    segment = segment_ids.astype(F32)
    segments_all = gather_batch(segment_ids)
    local_index = routed[0] - batch_index * token_count
    is_mine = (local_index >= 0) & (local_index < token_count)
    pick = (local_index[:, None] == jnp.arange(token_count)[None, :]).astype(F32)
    slot_grads = lax.psum(jnp.einsum("st,td->sd", pick, cotangent, precision=HIGHEST), BATCH)
    slot_segments = segments_all[routed[0]]

    heads_local = head_shards(masters)
    heads_dense = lax.all_gather(heads_local[0], FSDP, axis=0, tiled=True)
    up_dense = lax.all_gather(up_master[0].astype(BF16), FSDP, axis=0, tiled=True)
    down_dense = lax.all_gather(down_master[0].astype(BF16), FSDP, axis=0, tiled=True)
    heads_routed = lax.all_gather(heads_local[1], FSDP, axis=0, tiled=True)
    up_routed = lax.all_gather(up_master[1].astype(BF16), FSDP, axis=0, tiled=True)
    down_routed = lax.all_gather(down_master[1].astype(BF16), FSDP, axis=0, tiled=True)

    moments_heads = jnp.concatenate([qkv_moment, out_moment], axis=2).reshape(
        2, 8, 4, N_BATCH, LOCAL_HEADS, HDIM
    )
    moments_heads = jnp.transpose(moments_heads, (0, 2, 4, 3, 1, 5)).reshape(128, 8, HDIM)
    moment_block = lax.all_to_all(
        moments_heads, EVERY, split_axis=0, concat_axis=0, tiled=True
    ).reshape(D, HDIM)

    normed_low = gather_batch(rms_norm(inputs).astype(BF16))
    projected = qkv_forward(normed_low, heads_dense)
    mixed_low, log_total = attend(projected, sequence_pos, segments_all)
    middle = inputs + scatter_batch(out_forward(mixed_low, heads_dense))
    normed_two = gather_batch(rms_norm(middle).astype(BF16))
    fed_part, feed_hidden, feed_active = feed_forward(normed_two, up_dense, down_dense)
    hidden = middle + scatter_batch(fed_part)

    slot_rows = lax.psum(jnp.einsum("st,td->sd", pick, hidden, precision=HIGHEST), BATCH)
    slot_normed = rms_norm(slot_rows)
    slot_low = slot_normed.astype(BF16)
    gate_values = jnp.dot(slot_normed, router, precision=HIGHEST)
    r_projected = qkv_forward(slot_low, heads_routed)
    r_mixed, r_log_total = attend(r_projected, slot_pos, slot_segments)
    r_attended = lax.psum(out_forward(r_mixed, heads_routed), BATCH)
    r_middle = slot_rows + r_attended
    r_two = rms_norm(r_middle).astype(BF16)
    r_fed_part, r_hidden, r_active = feed_forward(r_two, up_routed, down_routed)
    routed_branch = r_attended + lax.psum(r_fed_part, BATCH)
    update_rows = gate_values[:, None] * routed_branch
    mixed = hidden + jnp.einsum("st,sd->td", pick, update_rows, precision=HIGHEST)

    gate_grads = jnp.sum(slot_grads * routed_branch, axis=1)
    branch_grads = gate_values[:, None] * slot_grads
    r_grad_two, r_grad_up, r_grad_down = feed_backward(
        r_two, up_routed, down_routed, r_hidden, r_active, branch_grads.astype(BF16)
    )
    r_grad_mid = norm_back(r_middle, lax.psum(r_grad_two, BATCH))
    r_grad_normed, r_grad_heads = attention_grads(
        slot_low,
        heads_routed,
        r_mixed,
        r_projected,
        slot_pos,
        slot_segments,
        r_log_total,
        (r_grad_mid + branch_grads).astype(BF16),
    )
    r_grad_normed = lax.psum(r_grad_normed, BATCH)
    own_slots = slot_pos // (K_ROUTE // N_BATCH) == batch_index
    router_grad = jnp.dot(jnp.where(own_slots, gate_grads, 0.0), slot_normed, precision=HIGHEST)
    router_total = lax.psum(router_grad, EVERY)
    slot_input_grads = r_grad_mid + norm_back(
        slot_rows, r_grad_normed + gate_grads[:, None] * router[None, :]
    )
    hidden_grads = cotangent + jnp.einsum("st,sd->td", pick, slot_input_grads, precision=HIGHEST)

    dense_low = gather_batch(hidden_grads.astype(BF16))
    grad_two, grad_up, grad_down = feed_backward(
        normed_two, up_dense, down_dense, feed_hidden, feed_active, dense_low
    )
    grad_mid = hidden_grads + norm_back(middle, scatter_batch(grad_two))
    grad_normed, grad_heads = attention_grads(
        normed_low,
        heads_dense,
        mixed_low,
        projected,
        sequence_pos,
        segments_all,
        log_total,
        gather_batch(grad_mid.astype(BF16)),
    )
    grad_inputs = grad_mid + norm_back(inputs, scatter_batch(grad_normed))

    wide_grads = jnp.stack(
        [
            lax.psum_scatter(grads, FSDP, scatter_dimension=0, tiled=True)
            for grads in (grad_up, r_grad_up, grad_down, r_grad_down)
        ]
    )
    new_up_moment = MOMENTUM * up_moment + wide_grads[:2]
    new_down_moment = MOMENTUM * down_moment + wide_grads[2:]
    wide_own = jnp.concatenate([new_up_moment, new_down_moment], axis=0)
    wide_rows = lax.all_to_all(wide_own, "z", split_axis=0, concat_axis=0, tiled=True).reshape(128, D)
    wide_gram = lax.psum(
        jnp.einsum("rb,rc->bc", wide_rows, wide_rows, precision=HIGHEST), ("y", "x", "c")
    )
    wide_ortho = newton_two(wide_rows, wide_gram).reshape(4, 32, D)
    wide_ortho = lax.all_to_all(wide_ortho, "z", split_axis=0, concat_axis=0, tiled=True)

    def blocks_of(grads):
        return jnp.transpose(grads.reshape(D, 8, HDIM), (1, 0, 2))

    block_grads = jnp.concatenate([blocks_of(grad_heads), blocks_of(r_grad_heads)], axis=0)
    block_grad = lax.psum_scatter(
        block_grads.reshape(16, D * HDIM // 128, 128), FSDP, scatter_dimension=0, tiled=True
    ).reshape(D, HDIM)
    new_block = MOMENTUM * moment_block + block_grad
    ortho_block = newton_heads(new_block)
    returned = jnp.concatenate([new_block, ortho_block], axis=1).reshape(128, 8, 2 * HDIM)
    returned = lax.all_to_all(returned, EVERY, split_axis=0, concat_axis=0, tiled=True)
    returned = returned.reshape(2, 4, LOCAL_HEADS, N_BATCH, 8, 2, HDIM)
    returned = jnp.transpose(returned, (5, 0, 4, 1, 3, 2, 6)).reshape(2, 2, 8, 4 * D)
    new_moments = (returned[0, :, :, : 3 * D], returned[0, :, :, 3 * D :], new_up_moment, new_down_moment)
    orthos = (returned[1, :, :, : 3 * D], returned[1, :, :, 3 * D :], wide_ortho[:2], wide_ortho[2:])

    widths = (HDIM, HDIM, D, D)
    full_rows = (D, D, FF, FF)
    new_masters = []
    for index_type in range(4):
        rate = STEP_RATES[index_type]
        factor = 0.2 * math.sqrt(max(full_rows[index_type], widths[index_type]))
        new_masters.append(
            masters[index_type] * (1.0 - rate * WEIGHT_DECAY) - rate * factor * orthos[index_type]
        )
    first_new = FIRST_DECAY * router_first + (1.0 - FIRST_DECAY) * router_total
    second_new = SECOND_DECAY * router_second + (1.0 - SECOND_DECAY) * router_total * router_total
    corrected_first = first_new / (1.0 - FIRST_DECAY**STEP)
    corrected_second = second_new / (1.0 - SECOND_DECAY**STEP)
    router_new = router * (1.0 - ADAM_RATE * WEIGHT_DECAY) - ADAM_RATE * corrected_first / (
        jnp.sqrt(corrected_second) + ADAM_EPSILON
    )
    return (
        (mixed, grad_inputs)
        + new_moments
        + tuple(new_masters)
        + tuple(master.astype(BF16) for master in new_masters)
        + (router_new, first_new, second_new)
    )


def solution(mesh):
    fine = Mesh(mesh.devices.reshape(4, 4, 4, 2), EVERY)
    tokens = P(EVERY, None)
    weights = P(None, EVERY, None)
    return jax.shard_map(
        body,
        mesh=fine,
        in_specs=(tokens, tokens, P(EVERY), P(FSDP, None)) + (weights,) * 8 + (P(),) * 3,
        out_specs=(tokens, tokens) + (weights,) * 12 + (P(),) * 3,
        check_vma=False,
    )
```

```python
import functools
import math

import jax
import jax.numpy as jnp
from jax import lax
from jax.experimental import pallas as pl
from jax.experimental.pallas import tpu as pltpu
from jax.sharding import Mesh
from jax.sharding import PartitionSpec as P

D = 1024
HEADS = 16
HDIM = 64
FF = 4096
STEP = 8
N_FSDP = 16
N_BATCH = 8
LOCAL_HEADS = HEADS // N_BATCH
LOCAL_WIDTH = LOCAL_HEADS * HDIM
K_ROUTE = 256

EPSILON = 1e-05
SCORE_SCALE = 0.125
NEGATIVE = -1e30
MOMENTUM = 0.95
WEIGHT_DECAY = 0.01
STEP_RATES = (0.15, 1.0, 0.15, 0.15)
NEWTON_A = 3.4445
NEWTON_B = -4.775
NEWTON_C = 2.0315
NEWTON_EPSILON = 1e-07
ADAM_RATE = 0.03
FIRST_DECAY = 0.9
SECOND_DECAY = 0.95
ADAM_EPSILON = 1e-08
HIGHEST = lax.Precision.HIGHEST
F32 = jnp.float32
BF16 = jnp.bfloat16

FSDP = ("y", "x")
BATCH = ("z", "c")
EVERY = ("y", "x", "z", "c")


def rms_norm(values):
    return values * lax.rsqrt(jnp.mean(values * values, axis=-1, keepdims=True) + EPSILON)


def gelu_tanh(values):
    return jax.nn.gelu(values, approximate=True)


def norm_back(values, grad_normed):
    pull_back = jax.vjp(rms_norm, values)[1]
    return pull_back(grad_normed)[0]


def dot_f32(pattern, left, right):
    return jnp.einsum(pattern, left, right, preferred_element_type=F32)


def shift(values, axis, step):
    size = 2 if axis == "c" else 4
    return lax.ppermute(values, axis, [(i, (i + step) % size) for i in range(size)])


def pair(values, axis, partner):
    return lax.ppermute(values, axis, [(i, partner(i)) for i in range(4)])


def neighbour_a(i):
    return i ^ 1


def neighbour_b(i):
    return 3 - i


def after(values, *others):
    return lax.optimization_barrier((values,) + others)[0]


def take(values, index):
    return lax.dynamic_index_in_dim(values, index, 0, keepdims=False)


def put(values, piece, index):
    return lax.dynamic_update_index_in_dim(values, piece, index, 0)


def turn(values, step, last=False):
    pairs = []
    for y in range(4):
        for x in range(4):
            for core in range(2):
                along_x = (core == 0) != last
                to_y, to_x = (y, (x + step) % 4) if along_x else ((y + step) % 4, x)
                pairs.append(((y * 4 + x) * 2 + core, (to_y * 4 + to_x) * 2 + core))
    return lax.ppermute(values, ("y", "x", "c"), pairs)


def turn_place(last=False):
    along_x = (lax.axis_index("c") == 0) != last
    return jnp.where(along_x, lax.axis_index("x"), lax.axis_index("y"))


def copy_rows(target, start, source, first, rows):
    step = min(rows, 64)

    @pl.loop(0, rows // step)
    def _(at):
        here = pl.ds(pl.multiple_of(first + at * step, step), step)
        there = pl.ds(pl.multiple_of(start + at * step, step), step)
        target[there, :] = source[here, :].astype(target.dtype)


def place_kernel(piece_count, sub_count, spots, *refs):
    pieces, whole = refs[:piece_count], refs[piece_count]
    rows = pieces[0].shape[0] // sub_count
    for p in range(piece_count):
        for s in range(sub_count):
            start = pl.multiple_of(spots[p * sub_count + s] * rows, rows)
            copy_rows(whole, start, pieces[p], s * rows, rows)


def place(pieces, spots, sub_count=1):
    rows = len(pieces) * pieces[0].shape[0]
    shape = (rows,) + pieces[0].shape[1:]
    size = math.prod(shape) * pieces[0].dtype.itemsize
    return pl.pallas_call(
        functools.partial(place_kernel, len(pieces), sub_count),
        out_shape=jax.ShapeDtypeStruct(shape, pieces[0].dtype),
        in_specs=[IN_SMEM] + [IN_VMEM] * len(pieces),
        out_specs=IN_VMEM,
        compiler_params=pltpu.CompilerParams(vmem_limit_bytes=40 * 2**20),
        cost_estimate=pl.CostEstimate(flops=0, bytes_accessed=2 * size, transcendentals=0),
    )(spots, *pieces)


def split_kernel(rows, spots, up, down, *outs):
    for step in range(4):
        for i in range(4):
            first = pl.multiple_of(spots[4 * step + i] * rows, rows)
            copy_rows(outs[step], 2 * i * rows, up, first, rows)
            copy_rows(outs[step], (2 * i + 1) * rows, down, first, rows)


def split(up, down, spots):
    rows = up.shape[0] // 16
    shape = jax.ShapeDtypeStruct((8 * rows, up.shape[1]), BF16)
    return pl.pallas_call(
        functools.partial(split_kernel, rows),
        out_shape=(shape,) * 4,
        in_specs=[IN_SMEM, IN_VMEM, IN_VMEM],
        out_specs=(IN_VMEM,) * 4,
        compiler_params=pltpu.CompilerParams(vmem_limit_bytes=40 * 2**20),
        cost_estimate=pl.CostEstimate(flops=0, bytes_accessed=3 * up.size * 4, transcendentals=0),
    )(spots, up, down)


IN_VMEM = pl.BlockSpec(memory_space=pltpu.VMEM)
IN_SMEM = pl.BlockSpec(memory_space=pltpu.SMEM)


def in_line(pieces):
    return place(pieces, jnp.arange(len(pieces), dtype=jnp.int32))


def gather_fsdp(values):
    core = lax.axis_index("c")
    mine, far = turn_place(), turn_place(True)
    line = in_line([values] + [turn(values, step) for step in (1, 2, 3)])
    pieces = [line] + [turn(line, step, True) for step in (1, 2, 3)]
    step = jnp.arange(4)
    first, second = (mine - step[None, :]) % 4, (far - step[:, None]) % 4
    spots = jnp.where(core == 0, second * 4 + first, first * 4 + second)
    return place(pieces, spots.reshape(16).astype(jnp.int32), 4)


def turn_parts(parts, last=False):
    me = turn_place(last)
    parts = parts.reshape((4, -1) + parts.shape[1:])
    sent = tuple(take(parts, (me + step) % 4).astype(BF16) for step in (1, 2, 3))
    own = take(parts, me).astype(F32)
    return (own,) + sent, tuple(turn(sent[i], i + 1, last) for i in range(3))


def turn_total(state):
    total = state[0][0].astype(F32)
    for piece in state[1]:
        total = total + piece.astype(F32)
    return total


def scatter_fsdp_first(up, down):
    core = lax.axis_index("c")
    me = turn_place()
    step, other = jnp.arange(4)[:, None], jnp.arange(4)[None, :]
    spot = (me + step) % 4
    spots = jnp.where(core == 0, other * 4 + spot, spot * 4 + other)
    parts = split(up, down, spots.reshape(16).astype(jnp.int32))
    return tuple(parts), tuple(turn(parts[step], step) for step in (1, 2, 3))


def scatter_fsdp_second(state):
    return turn_parts(turn_total(state), True)


def scatter_fsdp_value(state):
    total = turn_total(state)
    return total.reshape(2, -1, total.shape[1])


def turn_first(values):
    return turn_parts(values)


def turn_second(state):
    return turn_parts(turn_total(state), True)


def turn_third(state):
    total = turn_total(state).astype(BF16)
    return (total,), tuple(turn(total, step, True) for step in (1, 2, 3))


def turn_fourth(state):
    spots = (turn_place(True) - jnp.arange(4)) % 4
    line = place([state[0][0], *state[1]], spots.astype(jnp.int32))
    return (line,), tuple(turn(line, step) for step in (1, 2, 3))


def turn_value(state):
    spots = (turn_place() - jnp.arange(4)) % 4
    return place([state[0][0], *state[1]], spots.astype(jnp.int32))


def place_columns_kernel(width, spots, *refs):
    pieces, whole = refs[:-1], refs[-1]
    for p, piece in enumerate(pieces):
        for s in range(piece.shape[1] // width):
            start = pl.multiple_of(spots[p * (piece.shape[1] // width) + s] * width, width)
            whole[:, pl.ds(start, width)] = piece[:, s * width : (s + 1) * width]


def place_columns(pieces, spots):
    rows, width = pieces[0].shape
    return pl.pallas_call(
        functools.partial(place_columns_kernel, LOCAL_WIDTH),
        out_shape=jax.ShapeDtypeStruct((rows, width * len(pieces)), pieces[0].dtype),
        in_specs=[IN_SMEM] + [IN_VMEM] * len(pieces),
        out_specs=IN_VMEM,
        cost_estimate=pl.CostEstimate(flops=0, bytes_accessed=2**20, transcendentals=0),
    )(spots, *pieces)


def take_columns_kernel(width, spots, values, kept, given):
    rows = values.shape[0]
    for step in range(4):
        for i, out in enumerate((kept, given)):
            start = pl.multiple_of(spots[2 * step + i] * width, width)
            out[step * rows : (step + 1) * rows, :] = values[:, pl.ds(start, width)]


def take_columns(values, spots):
    shape = jax.ShapeDtypeStruct((4 * values.shape[0], LOCAL_WIDTH), values.dtype)
    return pl.pallas_call(
        functools.partial(take_columns_kernel, LOCAL_WIDTH),
        out_shape=(shape, shape),
        in_specs=[IN_SMEM, IN_VMEM],
        out_specs=(IN_VMEM, IN_VMEM),
        cost_estimate=pl.CostEstimate(flops=0, bytes_accessed=2**20, transcendentals=0),
    )(spots, values)


def during(state, work):
    sent, comes = state
    done = work(lambda values: after(values, *sent))
    leaves = jax.tree.leaves(done)
    comes = lax.optimization_barrier(tuple(comes) + tuple(leaves))[: len(comes)]
    return (sent, tuple(comes)), done


def gather_near(values):
    return (values,), (shift(values, "z", 1), shift(values, "z", -1))


def gather_far(state):
    (values,), (before, following) = state
    half = values.shape[0] // 2
    across = (shift(before[:half], "z", 1), shift(following[half:], "z", -1))
    return (values, before, following), across


def gather_core(state):
    (values, before, following), (low, high) = state
    half = values.shape[0] // 2
    pieces = [values[:half], values[half:], following[:half], following[half:], low, high]
    mine = in_line(pieces + [before[:half], before[half:]])
    return (mine,), (shift(mine, "c", 1),)


def gather_value(state):
    return in_line([state[0][0], state[1][0]])


def gather_batch(values):
    return gather_value(gather_core(gather_far(gather_near(values))))


def scatter_core(parts):
    rows = parts.shape[0] // 2
    given = parts[rows:].astype(BF16)
    return (parts, given), (shift(given, "c", 1),)


def scatter_far(state):
    (parts, _), (theirs,) = state
    rows = parts.shape[0] // 8
    half = rows // 2

    def mine(step, start, count):
        spot = step * rows + start
        return parts[spot : spot + count] + theirs[spot : spot + count].astype(F32)

    low, high = mine(2, 0, half).astype(BF16), mine(2, half, half).astype(BF16)
    near = (mine(0, 0, rows), mine(1, 0, rows), mine(3, 0, rows))
    return (low, high) + near, (shift(low, "z", 1), shift(high, "z", -1))


def scatter_near(state):
    (_, _, own, up, down), (low, high) = state
    half = low.shape[0]
    up = jnp.concatenate([up[:half] + low.astype(F32), up[half:]], axis=0).astype(BF16)
    down = jnp.concatenate([down[:half], down[half:] + high.astype(F32)], axis=0).astype(BF16)
    return (own, up, down), (shift(up, "z", 1), shift(down, "z", -1))


def scatter_value(state):
    return state[0][0] + state[1][0].astype(F32) + state[1][1].astype(F32)


def column_spots():
    at = jnp.arange(N_BATCH)
    core, place_z = lax.axis_index("c"), lax.axis_index("z")
    return (2 * ((place_z - at // 2) % 4) + (at + core) % 2).astype(jnp.int32)


def columns_core(values):
    return (values,), (shift(values, "c", 1),)


def columns_near(state):
    both = jnp.concatenate([state[0][0], state[1][0]], axis=1)
    return (both,), tuple(shift(both, "z", step) for step in (1, 2, 3))


def columns_value(state):
    return place_columns([state[0][0], *state[1]], column_spots())


def rows_core(values):
    half = values.shape[0] // 2
    given = values[half:]
    return (values, given), (shift(given, "c", 1),)


def rows_near(state):
    values, got = state[0][0], state[1][0]
    rows = values.shape[0] // 8
    pieces = []
    for step in range(4):
        spot = slice(step * rows, (step + 1) * rows)
        pieces.append(jnp.concatenate([values[spot], got[spot]], axis=1))
    return tuple(pieces), tuple(shift(pieces[step], "z", step) for step in (1, 2, 3))


def back_core(values):
    kept, given = take_columns(values, column_spots())
    return (kept, given), (shift(given, "c", 1),)


def back_near(state):
    kept, got = state[0][0], state[1][0]
    rows = kept.shape[0] // 4
    pieces = []
    for step in range(4):
        spot = slice(step * rows, (step + 1) * rows)
        pieces.append(jnp.concatenate([kept[spot], got[spot]], axis=0))
    return tuple(pieces), tuple(shift(pieces[step], "z", -step) for step in (1, 2, 3))


def back_value(state):
    pieces = (state[0][0],) + state[1]
    rows = pieces[0].shape[0] // 2
    return jnp.concatenate([piece[:rows] for piece in pieces] + [piece[rows:] for piece in pieces], axis=0)


def add(left, right):
    return left.astype(F32) + right.astype(F32)


def sum_core(values, kind=BF16):
    core = lax.axis_index("c")
    halves = values.reshape((2, values.shape[0] // 2) + values.shape[1:])
    given = take(halves, 1 - core).astype(kind)
    return (take(halves, core), given), (shift(given, "c", 1),)


def sum_near(state):
    (kept, given), (got,) = state
    kept = add(kept, got).astype(given.dtype)
    quarter = kept.shape[0] // 2
    low, high = kept[:quarter], kept[quarter:]
    return (low, high), (pair(low, "z", neighbour_a), pair(high, "z", neighbour_b))


def sum_next(state):
    (low, high), (from_low, from_high) = state
    low, high = add(low, from_low).astype(low.dtype), add(high, from_high).astype(high.dtype)
    return (low, high), (pair(low, "z", neighbour_b), pair(high, "z", neighbour_a))


def sum_last(state):
    (low, high), (from_low, from_high) = state
    kept = jnp.concatenate([add(low, from_low), add(high, from_high)], axis=0).astype(low.dtype)
    return (kept,), (shift(kept, "c", 1),)


def sum_value(state):
    core = lax.axis_index("c")
    kept, other = state[0][0].astype(F32), state[1][0].astype(F32)
    return jnp.concatenate(
        [jnp.where(core == 0, kept, other), jnp.where(core == 0, other, kept)], axis=0
    )


def head_shards(masters):
    joined = jnp.concatenate([masters[0].astype(BF16), masters[1].astype(BF16)], axis=2)
    parts = joined.reshape(2, 8, 4, N_BATCH, LOCAL_WIDTH)
    parts = jnp.transpose(parts, (3, 0, 1, 2, 4)).reshape(N_BATCH, 2, 8, 4 * LOCAL_WIDTH)
    moved = lax.all_to_all(parts, BATCH, split_axis=0, concat_axis=0, tiled=True)
    return jnp.transpose(moved, (1, 0, 2, 3)).reshape(2, 64, 4 * LOCAL_WIDTH)


BLOCK = 256


def masked_scores(keys, queries, key_block, query_block, key_segs, query_segs):
    scores = lax.dot_general(keys, queries, (((1,), (1,)), ((), ())), preferred_element_type=F32)
    key_pos = key_block * BLOCK + lax.broadcasted_iota(jnp.int32, (BLOCK, BLOCK), 0)
    query_pos = query_block * BLOCK + lax.broadcasted_iota(jnp.int32, (BLOCK, BLOCK), 1)
    allowed = (key_pos <= query_pos) & (key_segs == query_segs)
    return jnp.where(allowed, scores * SCORE_SCALE, NEGATIVE)


def head_columns(part, head):
    start = part * LOCAL_WIDTH + head * HDIM
    return slice(start, start + HDIM)


def attend_kernel(order, qkv, seg_row, seg_col, mixed, mixed_line, logs, keys, values_t, scores):
    block = pl.program_id(0)
    count = pl.num_programs(0)

    @pl.when(block == 0)
    def _():
        @pl.loop(0, count)
        def _(at):
            here = pl.ds(pl.multiple_of(at * BLOCK, BLOCK), BLOCK)
            rows = pl.ds(pl.multiple_of(order[at] * BLOCK, BLOCK), BLOCK)
            keys[here, :] = qkv[rows, LOCAL_WIDTH : 2 * LOCAL_WIDTH]
            values_t[:, here] = qkv[rows, 2 * LOCAL_WIDTH :].T

    here = pl.ds(pl.multiple_of(block * BLOCK, BLOCK), BLOCK)
    rows = pl.ds(pl.multiple_of(order[block] * BLOCK, BLOCK), BLOCK)
    query_segs = seg_row[:, here]
    heads = range(LOCAL_HEADS)
    queries = [qkv[rows, head_columns(0, head)] for head in heads]

    def score_step(at, tops):
        spot = pl.ds(pl.multiple_of(at * BLOCK, BLOCK), BLOCK)
        new = []
        for head in heads:
            found = masked_scores(
                keys[spot, head_columns(0, head)], queries[head], at, block, seg_col[spot, :], query_segs
            )
            scores[head, spot, :] = found
            new.append(jnp.maximum(tops[head], jnp.max(found, axis=0, keepdims=True)))
        return tuple(new)

    lowest = jnp.full((1, BLOCK), NEGATIVE, F32)
    tops = lax.fori_loop(0, block + 1, score_step, (lowest,) * LOCAL_HEADS)

    def exponent_step(at, totals):
        spot = pl.ds(pl.multiple_of(at * BLOCK, BLOCK), BLOCK)
        new = []
        for head in heads:
            exponent = jnp.exp(scores[head, spot, :] - tops[head])
            scores[head, spot, :] = exponent
            new.append(totals[head] + jnp.sum(exponent, axis=0, keepdims=True))
        return tuple(new)

    zero = jnp.zeros((1, BLOCK), F32)
    totals = lax.fori_loop(0, block + 1, exponent_step, (zero,) * LOCAL_HEADS)
    scales = [1.0 / total for total in totals]

    def value_step(at, sums):
        spot = pl.ds(pl.multiple_of(at * BLOCK, BLOCK), BLOCK)
        new = []
        for head in heads:
            probs = (scores[head, spot, :] * scales[head]).astype(BF16)
            new.append(
                sums[head]
                + jnp.dot(values_t[head_columns(0, head), spot], probs, preferred_element_type=F32)
            )
        return tuple(new)

    empty = jnp.zeros((HDIM, BLOCK), F32)
    sums = lax.fori_loop(0, block + 1, value_step, (empty,) * LOCAL_HEADS)
    result = jnp.concatenate(sums, axis=0).T.astype(BF16)
    mixed[rows, :] = result
    mixed_line[here, :] = result
    for head in heads:
        logs[head : head + 1, here] = tops[head] + jnp.log(totals[head])


def attend_back_kernel(
    order, qkv, grads, logs, seg_row, seg_col, out, out_line, keys, keys_t, values, grad_k, grad_v, probs, grad_probs
):
    block = pl.program_id(0)
    count = pl.num_programs(0)

    @pl.when(block == 0)
    def _():
        grad_k[...] = jnp.zeros_like(grad_k)
        grad_v[...] = jnp.zeros_like(grad_v)

        @pl.loop(0, count)
        def _(at):
            here = pl.ds(pl.multiple_of(at * BLOCK, BLOCK), BLOCK)
            rows = pl.ds(pl.multiple_of(order[at] * BLOCK, BLOCK), BLOCK)
            found = qkv[rows, LOCAL_WIDTH : 2 * LOCAL_WIDTH]
            keys[here, :] = found
            keys_t[:, here] = found.T
            values[here, :] = qkv[rows, 2 * LOCAL_WIDTH :]

    here = pl.ds(pl.multiple_of(block * BLOCK, BLOCK), BLOCK)
    rows = pl.ds(pl.multiple_of(order[block] * BLOCK, BLOCK), BLOCK)
    query_segs = seg_row[:, here]
    heads = range(LOCAL_HEADS)
    queries = [qkv[rows, head_columns(0, head)] for head in heads]
    grads_here = [grads[rows, head_columns(0, head)] for head in heads]
    logs_here = [logs[head : head + 1, here] for head in heads]

    def score_step(at, inners):
        spot = pl.ds(pl.multiple_of(at * BLOCK, BLOCK), BLOCK)
        new = []
        for head in heads:
            found = masked_scores(
                keys[spot, head_columns(0, head)], queries[head], at, block, seg_col[spot, :], query_segs
            )
            found = jnp.exp(found - logs_here[head])
            reached = lax.dot_general(
                values[spot, head_columns(0, head)],
                grads_here[head],
                (((1,), (1,)), ((), ())),
                preferred_element_type=F32,
            )
            probs[head, spot, :] = found
            grad_probs[head, spot, :] = reached
            new.append(inners[head] + jnp.sum(found * reached, axis=0, keepdims=True))
        return tuple(new)

    zero = jnp.zeros((1, BLOCK), F32)
    inners = lax.fori_loop(0, block + 1, score_step, (zero,) * LOCAL_HEADS)

    def grad_step(at, sums):
        spot = pl.ds(pl.multiple_of(at * BLOCK, BLOCK), BLOCK)
        new = []
        for head in heads:
            found = probs[head, spot, :]
            grad_scores = (found * (grad_probs[head, spot, :] - inners[head])).astype(BF16)
            grad_k[head, spot, :] += jnp.dot(grad_scores, queries[head], preferred_element_type=F32)
            grad_v[head, spot, :] += jnp.dot(
                found.astype(BF16), grads_here[head], preferred_element_type=F32
            )
            new.append(
                sums[head]
                + jnp.dot(keys_t[head_columns(0, head), spot], grad_scores, preferred_element_type=F32)
            )
        return tuple(new)

    empty = jnp.zeros((HDIM, BLOCK), F32)
    sums = lax.fori_loop(0, block + 1, grad_step, (empty,) * LOCAL_HEADS)
    result = (jnp.concatenate(sums, axis=0) * SCORE_SCALE).T.astype(BF16)
    out[rows, :LOCAL_WIDTH] = result
    out_line[here, :LOCAL_WIDTH] = result

    @pl.when(block == count - 1)
    def _():
        @pl.loop(0, count)
        def _(at):
            here = pl.ds(pl.multiple_of(at * BLOCK, BLOCK), BLOCK)
            rows = pl.ds(pl.multiple_of(order[at] * BLOCK, BLOCK), BLOCK)
            for head in heads:
                for part, found in ((1, grad_k[head, here, :] * SCORE_SCALE), (2, grad_v[head, here, :])):
                    out[rows, head_columns(part, head)] = found.astype(BF16)
                    out_line[here, head_columns(part, head)] = found.astype(BF16)


def skip_awaited(kernel, used, count, *refs):
    kernel(*refs[:used], *refs[used + count :])


def attend(projected, order, segments, *awaited):
    rows = projected.shape[0]
    return pl.pallas_call(
        functools.partial(skip_awaited, attend_kernel, 4, len(awaited)),
        grid=(rows // BLOCK,),
        out_shape=(
            jax.ShapeDtypeStruct((rows, LOCAL_WIDTH), BF16),
            jax.ShapeDtypeStruct((rows, LOCAL_WIDTH), BF16),
            jax.ShapeDtypeStruct((LOCAL_HEADS, rows), F32),
        ),
        in_specs=[IN_SMEM] + [IN_VMEM] * 3 + [pl.BlockSpec(memory_space=pl.ANY)] * len(awaited),
        out_specs=(IN_VMEM,) * 3,
        scratch_shapes=[
            pltpu.VMEM((rows, LOCAL_WIDTH), BF16),
            pltpu.VMEM((LOCAL_WIDTH, rows), BF16),
            pltpu.VMEM((LOCAL_HEADS, rows, BLOCK), F32),
        ],
        compiler_params=pltpu.CompilerParams(vmem_limit_bytes=40 * 2**20),
        cost_estimate=pl.CostEstimate(flops=rows, bytes_accessed=rows, transcendentals=0),
    )(order, projected, segments[None, :], segments[:, None], *awaited)


def attend_back(projected, order, segments, log_total, grad_mixed, *awaited):
    rows = projected.shape[0]
    return pl.pallas_call(
        functools.partial(skip_awaited, attend_back_kernel, 6, len(awaited)),
        grid=(rows // BLOCK,),
        out_shape=(jax.ShapeDtypeStruct((rows, 3 * LOCAL_WIDTH), BF16),) * 2,
        in_specs=[IN_SMEM] + [IN_VMEM] * 5 + [pl.BlockSpec(memory_space=pl.ANY)] * len(awaited),
        out_specs=(IN_VMEM,) * 2,
        scratch_shapes=[
            pltpu.VMEM((rows, LOCAL_WIDTH), BF16),
            pltpu.VMEM((LOCAL_WIDTH, rows), BF16),
            pltpu.VMEM((rows, LOCAL_WIDTH), BF16),
            pltpu.VMEM((LOCAL_HEADS, rows, HDIM), F32),
            pltpu.VMEM((LOCAL_HEADS, rows, HDIM), F32),
            pltpu.VMEM((LOCAL_HEADS, rows, BLOCK), F32),
            pltpu.VMEM((LOCAL_HEADS, rows, BLOCK), F32),
        ],
        compiler_params=pltpu.CompilerParams(vmem_limit_bytes=40 * 2**20),
        cost_estimate=pl.CostEstimate(flops=rows, bytes_accessed=rows, transcendentals=0),
    )(order, projected, grad_mixed, log_total, segments[None, :], segments[:, None], *awaited)


def qkv_forward(normed_all, weight_heads):
    return dot_f32("td,dc->tc", normed_all, weight_heads[:, : 3 * LOCAL_WIDTH]).astype(BF16)


def out_forward(mixed, weight_heads):
    return dot_f32("td,od->to", mixed, weight_heads[:, 3 * LOCAL_WIDTH :])


def feed_forward(normed_all, weight_up, weight_down):
    hidden = dot_f32("td,fd->tf", normed_all, weight_up)
    active = gelu_tanh(hidden).astype(BF16)
    return dot_f32("tf,fd->td", active, weight_down), hidden, active


def feed_backward(weight_up, weight_down, hidden, grad_low):
    grad_active = dot_f32("td,fd->tf", grad_low, weight_down)
    grad_hidden = jax.vjp(gelu_tanh, hidden)[1](grad_active)[0].astype(BF16)
    return grad_hidden, dot_f32("tf,fd->td", grad_hidden, weight_up)


def times(rows, gram):
    return jnp.dot(rows.astype(BF16), gram, preferred_element_type=F32)


def newton_two(rows, gram, scale):
    def polynomial(values):
        once = times(values, gram)
        return NEWTON_A * values + NEWTON_B * once + NEWTON_C * times(once, gram)

    first = polynomial(rows / scale)
    once = polynomial(times(polynomial(first), gram))
    twice = polynomial(times(polynomial(once), gram))
    return NEWTON_A * first + NEWTON_B * once + NEWTON_C * twice


def exact(left, right):
    return jnp.dot(left, right, precision=HIGHEST)


def newton_heads(block):
    gram = jnp.einsum("br,cr->bc", block, block, precision=HIGHEST)
    scale = jnp.sqrt(jnp.trace(gram)) + NEWTON_EPSILON
    gram = gram / (scale * scale)
    one = jnp.eye(HDIM, dtype=F32)
    first = NEWTON_A * one + NEWTON_B * gram + NEWTON_C * exact(gram, gram)
    gram = exact(exact(first, gram), first)
    second = NEWTON_A * one + NEWTON_B * gram + NEWTON_C * exact(gram, gram)
    return exact(exact(second, first), block / scale)


def body(
    inputs,
    cotangent,
    segment_ids,
    routed,
    qkv_master,
    out_master,
    up_master,
    down_master,
    qkv_moment,
    out_moment,
    up_moment,
    down_moment,
    router,
    router_first,
    router_second,
):
    masters = (qkv_master, out_master, up_master, down_master)
    token_count = inputs.shape[0]
    core, place_z = lax.axis_index("c"), lax.axis_index("z")
    batch_index = 2 * place_z + core
    all_tokens = jnp.arange(token_count * N_BATCH)

    at = jnp.arange(N_BATCH)
    order = (4 * ((at + core) % 2) + (at // 2 - place_z) % 4).astype(jnp.int32)
    block_of = 2 * ((at % 4 + place_z) % 4) + (at // 4 + core) % 2
    row_pos = (block_of[:, None] * token_count + jnp.arange(token_count)[None, :]).reshape(-1)
    single = jnp.zeros((1,), jnp.int32)

    normed_round = gather_near(rms_norm(inputs).astype(BF16))
    heads_local = head_shards(masters)
    wide_dense = jnp.stack([up_master[0], down_master[0]]).astype(BF16)
    wide_dense = lax.all_gather(wide_dense, FSDP, axis=1, tiled=True)
    up_dense, down_dense = wide_dense[0], wide_dense[1]
    out_low = jnp.concatenate([out_master[0], out_master[1]], axis=1).astype(BF16)
    out_low = lax.all_gather(out_low, EVERY, axis=0, tiled=True)
    out_dense, out_routed = out_low[:, :D], out_low[:, D:]
    wide_routed = jnp.stack([up_master[1], down_master[1]]).astype(BF16)
    wide_routed = lax.all_gather(wide_routed, FSDP, axis=1, tiled=True)
    up_routed, down_routed = wide_routed[0], wide_routed[1]
    heads_dense = gather_fsdp(heads_local[0])
    normed_low = gather_value(gather_core(gather_far(normed_round)))

    chosen = routed[0]
    local_index = chosen - batch_index * token_count
    pick = (local_index[:, None] == jnp.arange(token_count)[None, :]).astype(F32)
    pick_all = (chosen[:, None] == row_pos[None, :]).astype(BF16)
    not_routed = 1.0 - jnp.max(pick, axis=0)[:, None]
    rest_grads = cotangent * not_routed
    segment_blocks = segment_ids.astype(F32)[None, :]
    segment_blocks = jnp.concatenate([segment_blocks, shift(segment_blocks, "c", 1)], axis=0)
    segment_blocks = jnp.concatenate(
        [segment_blocks] + [shift(segment_blocks, "z", step) for step in (1, 2, 3)], axis=0
    )
    segments_all = jnp.sum(
        jnp.where((column_spots()[:, None] == at[None, :])[:, :, None], segment_blocks[:, None, :], 0.0),
        axis=0,
    ).reshape(-1)
    slot_segments = jnp.sum(
        jnp.where(chosen[:, None] == all_tokens[None, :], segments_all[None, :], 0.0), axis=1
    )

    moments_heads = jnp.concatenate([qkv_moment, out_moment], axis=2).reshape(
        2, 8, 4, N_BATCH, LOCAL_HEADS, HDIM
    )
    moments_heads = jnp.transpose(moments_heads, (0, 2, 4, 3, 1, 5)).reshape(128, 8, HDIM)
    moment_block = lax.all_to_all(
        moments_heads, EVERY, split_axis=0, concat_axis=0, tiled=True
    ).reshape(D, HDIM)
    moment_block = jnp.transpose(moment_block)

    def of_slots(values):
        return jnp.einsum("st,td->sd", pick_all, values, preferred_element_type=F32).astype(BF16)

    start_rows = jnp.einsum("st,td->sd", pick, inputs, precision=HIGHEST)
    start_round = sum_near(sum_core(after(start_rows, *normed_round[1]), F32))
    slot_inputs = sum_value(sum_last(sum_next(start_round)))
    heads_routed = gather_fsdp(heads_local[1])
    projected = qkv_forward(normed_low, heads_dense)
    rest_round = gather_near(after(rest_grads.astype(BF16), normed_low))
    mixed_low, mixed_line, log_total = attend(
        projected, order, segments_all, moment_block, heads_routed, slot_inputs, rest_round[0][0]
    )
    mixed_slots = of_slots(mixed_low)

    slot_round = columns_core(mixed_slots)
    slot_round = columns_near(slot_round)
    slot_middle = slot_inputs + dot_f32("td,od->to", columns_value(slot_round), out_dense)
    slot_two = rms_norm(slot_middle).astype(BF16)
    slot_fed, slot_hidden, slot_active = feed_forward(slot_two, up_dense, down_dense)

    fed_round = sum_core(slot_fed)
    mixed_round = rows_core(after(mixed_low, *fed_round[0]))
    fed_round = sum_near(fed_round)
    mixed_round = rows_near(mixed_round)
    fed_round, mixed_rows = during(fed_round, lambda late: columns_value(mixed_round))
    fed_round = sum_next(fed_round)

    def rest_forward(late):
        middle = inputs + dot_f32("td,od->to", late(mixed_rows), out_dense)
        return middle, rms_norm(middle).astype(BF16)

    fed_round, (middle, rest_two_low) = during(fed_round, rest_forward)
    fed_round = sum_last(fed_round)
    two_round = gather_near(after(rest_two_low, *fed_round[0]))
    slot_rows = slot_middle + sum_value(fed_round)

    slot_normed = rms_norm(slot_rows)
    slot_low = slot_normed.astype(BF16)
    r_projected = qkv_forward(slot_low, heads_routed)
    r_mixed, _, r_log_total = attend(r_projected, single, slot_segments)
    r_round = columns_core(r_mixed)
    gate_values = jnp.dot(slot_normed, router, precision=HIGHEST)
    r_round = columns_near(r_round)
    two_round = gather_far((two_round[0], lax.optimization_barrier(two_round[1] + r_round[0])[:2]))
    r_attended = dot_f32("td,od->to", columns_value(r_round), out_routed)
    r_middle = slot_rows + r_attended
    r_two = rms_norm(r_middle).astype(BF16)
    r_fed_part, r_hidden, r_active = feed_forward(r_two, up_routed, down_routed)
    rest_round = gather_far((rest_round[0], lax.optimization_barrier(rest_round[1] + (r_two,))[:2]))

    r_round = sum_core(r_fed_part)
    two_round = gather_core((two_round[0], lax.optimization_barrier(two_round[1] + r_round[0])[:2]))
    r_round = sum_near(r_round)
    r_round, normed_two = during(r_round, lambda late: gather_value(two_round))
    r_round = sum_next(r_round)

    def rest_active(late):
        _, hidden, active = feed_forward(late(normed_two), up_dense, down_dense)
        return hidden, active

    r_round, (feed_hidden, feed_active) = during(r_round, rest_active)
    rest_round = gather_core((rest_round[0], lax.optimization_barrier(rest_round[1] + (feed_active,))[:2]))
    r_round = sum_last(r_round)
    r_round, rest_low = during(r_round, lambda late: gather_value(rest_round))
    routed_branch = r_attended + sum_value(r_round)

    grads_round = sum_near(
        sum_core(after(jnp.einsum("st,td->sd", pick, cotangent, precision=HIGHEST), mixed_low), F32)
    )
    slot_grads = sum_value(sum_last(sum_next(grads_round)))
    branch_grads = gate_values[:, None] * slot_grads
    branch_low = branch_grads.astype(BF16)
    r_grad_hidden, r_grad_two = feed_backward(up_routed, down_routed, r_hidden, branch_low)

    r_round = sum_near(sum_core(r_grad_two))

    def rest_back(late):
        return feed_backward(up_dense, down_dense, feed_hidden, late(rest_low))

    r_round, (rest_hidden, rest_two) = during(r_round, rest_back)
    back_round = scatter_core(rest_two)
    r_round = sum_next(r_round)
    r_round, gate_grads = during(r_round, lambda late: jnp.sum(late(slot_grads) * routed_branch, axis=1))
    back_round = scatter_far((back_round[0], lax.optimization_barrier(back_round[1] + r_round[0])[:1]))
    r_round = sum_last(r_round)
    r_grad_mid = norm_back(r_middle, sum_value(r_round))
    r_grad_low = (r_grad_mid + branch_grads).astype(BF16)

    def out_back(grad_low, weight_heads):
        return dot_f32("to,od->td", grad_low, weight_heads[:, 3 * LOCAL_WIDTH :]).astype(BF16)

    r_grad_projected, _ = attend_back(
        r_projected, single, slot_segments, r_log_total, out_back(r_grad_low, heads_routed)
    )
    r_round = sum_core(dot_f32("tc,dc->td", r_grad_projected, heads_routed[:, : 3 * LOCAL_WIDTH]))
    back_round = scatter_near((back_round[0], lax.optimization_barrier(back_round[1] + r_round[0])[:2]))
    r_round = sum_near(r_round)

    def routed_weights(late):
        return (
            dot_f32("tf,td->fd", late(r_grad_hidden), r_two),
            dot_f32("tf,td->fd", r_active, late(branch_low)),
        )

    r_round, (r_grad_up, r_grad_down) = during(r_round, routed_weights)
    r_round = sum_next(r_round)

    def rest_middle(late):
        rest_mid = rest_grads + norm_back(middle, late(scatter_value(back_round)))
        rest_mid_low = rest_mid.astype(BF16)
        return rest_mid, rest_mid_low, dot_f32("to,od->td", rest_mid_low, out_dense).astype(BF16)

    r_round, (rest_mid, rest_mid_low, rest_mixed) = during(r_round, rest_middle)
    rest_mid_all = lax.all_gather(rest_mid_low, BATCH, axis=0, tiled=True)
    r_round = sum_last(r_round)
    back_round = back_core(after(rest_mixed, *r_round[0]))
    r_grad_normed = sum_value(r_round)
    slot_out_grads = (
        slot_grads
        + r_grad_mid
        + norm_back(slot_rows, r_grad_normed + gate_grads[:, None] * router[None, :])
    )

    slot_out_low = slot_out_grads.astype(BF16)
    slot_grad_hidden, slot_grad_two = feed_backward(up_dense, down_dense, slot_hidden, slot_out_low)
    slot_round = sum_core(slot_grad_two)
    back_round = back_near((back_round[0], lax.optimization_barrier(back_round[1] + slot_round[0])[:1]))
    slot_round = sum_near(slot_round)
    slot_round, rest_up = during(
        slot_round, lambda late: dot_f32("tf,td->fd", late(rest_hidden), normed_two)
    )
    slot_round = sum_next(slot_round)
    slot_round, rest_down = during(
        slot_round, lambda late: dot_f32("tf,td->fd", feed_active, late(rest_low))
    )
    slot_round = sum_last(slot_round)
    slot_mid = slot_out_grads + norm_back(slot_middle, sum_value(slot_round))
    slot_mid_low = slot_mid.astype(BF16)
    slot_mixed = out_back(slot_mid_low, heads_dense)
    grad_mixed = (
        back_value(back_round).astype(F32)
        + jnp.einsum("st,sd->td", pick_all, slot_mixed, preferred_element_type=F32)
    ).astype(BF16)
    grad_up = rest_up + dot_f32("tf,td->fd", slot_grad_hidden, slot_two)
    grad_down = rest_down + dot_f32("tf,td->fd", slot_active, slot_out_low)
    wide_round = scatter_fsdp_first(grad_up, grad_down)
    grad_mixed = after(grad_mixed, *wide_round[0])
    grad_projected, grad_projected_line = attend_back(projected, order, segments_all, log_total, grad_mixed)

    routed_wide = lax.psum_scatter(
        jnp.stack([r_grad_up, r_grad_down]), FSDP, scatter_dimension=1, tiled=True
    )
    wide_round = (
        wide_round[0],
        lax.optimization_barrier(wide_round[1] + (grad_projected, routed_wide))[:3],
    )
    wide_round = scatter_fsdp_second(wide_round)

    def dense_weights(late):
        grads = late(grad_projected)
        grad_qkv = dot_f32("tc,td->cd", grads, normed_low)
        grad_out = dot_f32("td,to->do", mixed_line, rest_mid_all) + dot_f32(
            "td,to->do", mixed_slots, slot_mid_low
        )
        return grad_qkv, grad_out

    wide_round, (grad_qkv, grad_out) = during(wide_round, dense_weights)
    dense_wide = scatter_fsdp_value(wide_round)

    r_grad_qkv = dot_f32("tc,td->cd", r_grad_projected, slot_low)
    r_grad_out = dot_f32("td,to->do", r_mixed, r_grad_low)
    block_parts = jnp.concatenate([grad_qkv, grad_out, r_grad_qkv, r_grad_out], axis=0).astype(BF16)
    router_grad = jnp.dot(gate_grads, slot_normed, precision=HIGHEST)
    router_high = router_grad.astype(BF16)
    router_low = (router_grad - router_high.astype(F32)).astype(BF16)
    router_rows = jnp.concatenate(
        [router_high[None, :], router_low[None, :], jnp.zeros((14, D), BF16)], axis=0
    )
    block_parts = jnp.concatenate(
        [block_parts.reshape(16, HDIM, D), jnp.broadcast_to(router_rows[None], (16, 16, D))], axis=1
    )
    block_grads = lax.all_to_all(block_parts, FSDP, split_axis=0, concat_axis=0, tiled=True)

    new_up_moment = MOMENTUM * up_moment + jnp.stack([dense_wide[0], routed_wide[0]])
    new_down_moment = MOMENTUM * down_moment + jnp.stack([dense_wide[1], routed_wide[1]])
    wide_own = after(jnp.concatenate([new_up_moment, new_down_moment], axis=0), block_parts)
    wide_rows = lax.all_to_all(wide_own, "z", split_axis=0, concat_axis=0, tiled=True).reshape(128, D)
    grad_normed = dot_f32(
        "tc,dc->td", after(grad_projected_line, block_parts), heads_dense[:, : 3 * LOCAL_WIDTH]
    )
    rows_low = wide_rows.astype(BF16)
    rows_both = jnp.concatenate([rows_low, shift(rows_low, "c", 1)], axis=0)
    rows_both = after(rows_both, grad_normed, block_grads)
    grad_normed = lax.psum_scatter(grad_normed, BATCH, scatter_dimension=0, tiled=True)
    own_columns = lax.dynamic_slice_in_dim(rows_both, core * (D // 2), D // 2, 1)
    gram_part = dot_f32("rb,rc->bc", own_columns, rows_both)

    def heads_step(late):
        grads = jnp.sum(late(block_grads).astype(F32), axis=0)
        new_block = MOMENTUM * moment_block + grads[:HDIM]
        ortho_block = newton_heads(new_block)
        returned = jnp.transpose(jnp.concatenate([new_block, ortho_block], axis=0))
        return returned.reshape(128, 8, 2 * HDIM), grads[HDIM] + grads[HDIM + 1]

    def fed_step(late):
        spots = jnp.argsort(order).astype(jnp.int32)
        fed_line = place([late(feed_active)], spots, N_BATCH)
        return dot_f32("tf,fd->td", fed_line, down_dense)

    gram_round = turn_first(gram_part)
    gram_round, (returned, router_total) = during(gram_round, heads_step)
    gram_round = turn_second(gram_round)
    returned = lax.all_to_all(returned, EVERY, split_axis=0, concat_axis=0, tiled=True)
    gram_round = turn_third(gram_round)
    gram_round = turn_fourth(gram_round)
    gram_round, fed_line = during(gram_round, fed_step)
    fed_rows = lax.psum_scatter(after(fed_line, grad_normed), BATCH, scatter_dimension=0, tiled=True)
    gram_half = turn_value(gram_round)
    gram_other = shift(gram_half, "c", 1)
    wide_gram = jnp.concatenate(
        [jnp.where(core == 0, gram_half, gram_other), jnp.where(core == 0, gram_other, gram_half)],
        axis=0,
    )
    wide_scale = jnp.sqrt(jnp.trace(wide_gram.astype(F32))) + NEWTON_EPSILON
    wide_gram = (wide_gram.astype(F32) / (wide_scale * wide_scale)).astype(BF16)
    wide_ortho = newton_two(wide_rows, wide_gram, wide_scale).reshape(4, 32, D)
    wide_ortho = lax.all_to_all(wide_ortho, "z", split_axis=0, concat_axis=0, tiled=True)

    grad_mid = rest_mid + jnp.einsum("st,sd->td", pick, slot_mid, precision=HIGHEST)
    grad_inputs = grad_mid + norm_back(inputs, grad_normed)
    mixed = (
        middle
        + fed_rows
        + jnp.einsum("st,sd->td", pick, gate_values[:, None] * routed_branch, precision=HIGHEST)
    )

    returned = returned.reshape(2, 4, LOCAL_HEADS, N_BATCH, 8, 2, HDIM)
    returned = jnp.transpose(returned, (5, 0, 4, 1, 3, 2, 6)).reshape(2, 2, 8, 4 * D)
    new_moments = (returned[0, :, :, : 3 * D], returned[0, :, :, 3 * D :], new_up_moment, new_down_moment)
    orthos = (returned[1, :, :, : 3 * D], returned[1, :, :, 3 * D :], wide_ortho[:2], wide_ortho[2:])

    widths = (HDIM, HDIM, D, D)
    full_rows = (D, D, FF, FF)
    new_masters = []
    for index_type in range(4):
        rate = STEP_RATES[index_type]
        factor = 0.2 * math.sqrt(max(full_rows[index_type], widths[index_type]))
        new_masters.append(
            masters[index_type] * (1.0 - rate * WEIGHT_DECAY) - rate * factor * orthos[index_type]
        )
    first_new = FIRST_DECAY * router_first + (1.0 - FIRST_DECAY) * router_total
    second_new = SECOND_DECAY * router_second + (1.0 - SECOND_DECAY) * router_total * router_total
    corrected_first = first_new / (1.0 - FIRST_DECAY**STEP)
    corrected_second = second_new / (1.0 - SECOND_DECAY**STEP)
    router_new = router * (1.0 - ADAM_RATE * WEIGHT_DECAY) - ADAM_RATE * corrected_first / (
        jnp.sqrt(corrected_second) + ADAM_EPSILON
    )
    return (
        (mixed, grad_inputs)
        + new_moments
        + tuple(new_masters)
        + tuple(master.astype(BF16) for master in new_masters)
        + (router_new, first_new, second_new)
    )


def solution(mesh):
    fine = Mesh(mesh.devices.reshape(4, 4, 4, 2), EVERY)
    tokens = P(EVERY, None)
    weights = P(None, EVERY, None)
    return jax.shard_map(
        body,
        mesh=fine,
        in_specs=(tokens, tokens, P(EVERY), P(FSDP, None)) + (weights,) * 8 + (P(),) * 3,
        out_specs=(tokens, tokens) + (weights,) * 12 + (P(),) * 3,
        check_vma=False,
    )
```

```python
import functools
import math

import jax
import jax.numpy as jnp
from jax import lax
from jax.experimental import pallas as pl
from jax.experimental.pallas import tpu as pltpu
from jax.sharding import Mesh
from jax.sharding import PartitionSpec as P

D = 1024
HEADS = 16
HDIM = 64
FF = 4096
STEP = 8
N_FSDP = 16
N_BATCH = 8
LOCAL_HEADS = HEADS // N_BATCH
LOCAL_WIDTH = LOCAL_HEADS * HDIM
K_ROUTE = 256

EPSILON = 1e-05
SCORE_SCALE = 0.125
NEGATIVE = -1e30
MOMENTUM = 0.95
WEIGHT_DECAY = 0.01
STEP_RATES = (0.15, 1.0, 0.15, 0.15)
NEWTON_A = 3.4445
NEWTON_B = -4.775
NEWTON_C = 2.0315
NEWTON_EPSILON = 1e-07
ADAM_RATE = 0.03
FIRST_DECAY = 0.9
SECOND_DECAY = 0.95
ADAM_EPSILON = 1e-08
HIGHEST = lax.Precision.HIGHEST
F32 = jnp.float32
BF16 = jnp.bfloat16

FSDP = ("y", "x")
BATCH = ("z", "c")
EVERY = ("y", "x", "z", "c")

IN_VMEM = pl.BlockSpec(memory_space=pltpu.VMEM)
IN_SMEM = pl.BlockSpec(memory_space=pltpu.SMEM)


def rms_norm(values):
    return values * lax.rsqrt(jnp.mean(values * values, axis=-1, keepdims=True) + EPSILON)


def gelu_tanh(values):
    return jax.nn.gelu(values, approximate=True)


def norm_back(values, grad_normed):
    pull_back = jax.vjp(rms_norm, values)[1]
    return pull_back(grad_normed)[0]


def dot_f32(pattern, left, right):
    return jnp.einsum(pattern, left, right, preferred_element_type=F32)


def shift(values, axis, step):
    size = 2 if axis == "c" else 4
    return lax.ppermute(values, axis, [(i, (i + step) % size) for i in range(size)])


def pair(values, axis, partner):
    return lax.ppermute(values, axis, [(i, partner(i)) for i in range(4)])


def neighbour_a(i):
    return i ^ 1


def neighbour_b(i):
    return 3 - i


def after(values, *others):
    return lax.optimization_barrier((values,) + others)[0]


def take(values, index):
    return lax.dynamic_index_in_dim(values, index, 0, keepdims=False)


def put(values, piece, index):
    return lax.dynamic_update_index_in_dim(values, piece, index, 0)


def turn(values, step, last=False):
    pairs = []
    for y in range(4):
        for x in range(4):
            for core in range(2):
                along_x = (core == 0) != last
                to_y, to_x = (y, (x + step) % 4) if along_x else ((y + step) % 4, x)
                pairs.append(((y * 4 + x) * 2 + core, (to_y * 4 + to_x) * 2 + core))
    return lax.ppermute(values, ("y", "x", "c"), pairs)


def turn_place(last=False):
    along_x = (lax.axis_index("c") == 0) != last
    return jnp.where(along_x, lax.axis_index("x"), lax.axis_index("y"))


def copy_rows(target, start, source, first, rows):
    step = math.gcd(rows, 64)

    @pl.loop(0, rows // step)
    def _(at):
        here = pl.ds(pl.multiple_of(first + at * step, step), step)
        there = pl.ds(pl.multiple_of(start + at * step, step), step)
        target[there, :] = source[here, :].astype(target.dtype)


def place_kernel(piece_count, sub_count, spots, *refs):
    pieces, whole = refs[:piece_count], refs[piece_count]
    rows = pieces[0].shape[0] // sub_count
    for p in range(piece_count):
        for s in range(sub_count):
            start = pl.multiple_of(spots[p * sub_count + s] * rows, rows)
            copy_rows(whole, start, pieces[p], s * rows, rows)


def place(pieces, spots, sub_count=1):
    rows = len(pieces) * pieces[0].shape[0]
    shape = (rows,) + pieces[0].shape[1:]
    size = math.prod(shape) * pieces[0].dtype.itemsize
    return pl.pallas_call(
        functools.partial(place_kernel, len(pieces), sub_count),
        out_shape=jax.ShapeDtypeStruct(shape, pieces[0].dtype),
        in_specs=[IN_SMEM] + [IN_VMEM] * len(pieces),
        out_specs=IN_VMEM,
        compiler_params=pltpu.CompilerParams(vmem_limit_bytes=40 * 2**20),
        cost_estimate=pl.CostEstimate(flops=0, bytes_accessed=2 * size, transcendentals=0),
    )(spots, *pieces)


def split_kernel(rows, count, spots, *refs):
    values, outs = refs[:count], refs[count:]
    for step in range(4):
        for i in range(4):
            first = pl.multiple_of(spots[4 * step + i] * rows, rows)
            for at, source in enumerate(values):
                copy_rows(outs[step], (count * i + at) * rows, source, first, rows)


def split(values, spots):
    count = len(values)
    rows = values[0].shape[0] // 16
    shape = jax.ShapeDtypeStruct((4 * count * rows, values[0].shape[1]), BF16)
    return pl.pallas_call(
        functools.partial(split_kernel, rows, count),
        out_shape=(shape,) * 4,
        in_specs=[IN_SMEM] + [IN_VMEM] * count,
        out_specs=(IN_VMEM,) * 4,
        compiler_params=pltpu.CompilerParams(vmem_limit_bytes=40 * 2**20),
        cost_estimate=pl.CostEstimate(flops=0, bytes_accessed=2**22, transcendentals=0),
    )(spots, *values)


def in_line(pieces):
    return place(pieces, jnp.arange(len(pieces), dtype=jnp.int32))


def gather_fsdp_first(values):
    return (values,), tuple(turn(values, step) for step in (1, 2, 3))


def gather_fsdp_second(state):
    line = in_line([state[0][0], *state[1]])
    return (line,), tuple(turn(line, step, True) for step in (1, 2, 3))


def gather_fsdp_value(state):
    core = lax.axis_index("c")
    mine, far = turn_place(), turn_place(True)
    step = jnp.arange(4)
    first, second = (mine - step[None, :]) % 4, (far - step[:, None]) % 4
    spots = jnp.where(core == 0, second * 4 + first, first * 4 + second)
    return place([state[0][0], *state[1]], spots.reshape(16).astype(jnp.int32), 4)


def turn_parts(parts, last=False):
    me = turn_place(last)
    parts = parts.reshape((4, -1) + parts.shape[1:])
    sent = tuple(take(parts, (me + step) % 4).astype(BF16) for step in (1, 2, 3))
    own = take(parts, me).astype(F32)
    return (own,) + sent, tuple(turn(sent[i], i + 1, last) for i in range(3))


def turn_total(state):
    total = state[0][0].astype(F32)
    for piece in state[1]:
        total = total + piece.astype(F32)
    return total


def scatter_fsdp_first(*values):
    core = lax.axis_index("c")
    me = turn_place()
    step, other = jnp.arange(4)[:, None], jnp.arange(4)[None, :]
    spot = (me + step) % 4
    spots = jnp.where(core == 0, other * 4 + spot, spot * 4 + other)
    parts = split(values, spots.reshape(16).astype(jnp.int32))
    return tuple(parts), tuple(turn(parts[step], step) for step in (1, 2, 3))


def scatter_fsdp_second(state):
    return turn_parts(turn_total(state), True)


def exchange_near(values):
    place_z = lax.axis_index("z")
    pieces = tuple(take(values, (place_z + step) % 4) for step in range(4))
    return pieces, tuple(shift(pieces[step], "z", step) for step in (1, 2, 3))


def exchange_value(state):
    spots = (lax.axis_index("z") - jnp.arange(4)) % 4
    return place([state[0][0], *state[1]], spots.astype(jnp.int32))


def turn_first(values):
    return turn_parts(values)


def turn_second(state):
    return turn_parts(turn_total(state), True)


def turn_third(state):
    total = turn_total(state).astype(BF16)
    return (total,), tuple(turn(total, step, True) for step in (1, 2, 3))


def turn_fourth(state):
    spots = (turn_place(True) - jnp.arange(4)) % 4
    line = place([state[0][0], *state[1]], spots.astype(jnp.int32))
    return (line,), tuple(turn(line, step) for step in (1, 2, 3))


def turn_value(state):
    spots = (turn_place() - jnp.arange(4)) % 4
    return place([state[0][0], *state[1]], spots.astype(jnp.int32))


def place_columns_kernel(width, count, spots, *refs):
    pieces, whole = refs[:count], refs[-1]
    for p, piece in enumerate(pieces):
        for s in range(piece.shape[1] // width):
            start = pl.multiple_of(spots[p * (piece.shape[1] // width) + s] * width, width)
            whole[:, pl.ds(start, width)] = piece[:, s * width : (s + 1) * width]


def place_columns(pieces, spots, *awaited):
    rows, width = pieces[0].shape
    return pl.pallas_call(
        functools.partial(place_columns_kernel, LOCAL_WIDTH, len(pieces)),
        out_shape=jax.ShapeDtypeStruct((rows, width * len(pieces)), pieces[0].dtype),
        in_specs=[IN_SMEM]
        + [IN_VMEM] * len(pieces)
        + [pl.BlockSpec(memory_space=pl.ANY)] * len(awaited),
        out_specs=IN_VMEM,
        cost_estimate=pl.CostEstimate(flops=0, bytes_accessed=2**20, transcendentals=0),
    )(spots, *pieces, *awaited)


def take_columns_kernel(width, spots, values, kept, given):
    rows = values.shape[0]
    for step in range(4):
        for i, out in enumerate((kept, given)):
            start = pl.multiple_of(spots[2 * step + i] * width, width)
            out[step * rows : (step + 1) * rows, :] = values[:, pl.ds(start, width)]


def take_columns(values, spots):
    shape = jax.ShapeDtypeStruct((4 * values.shape[0], LOCAL_WIDTH), values.dtype)
    return pl.pallas_call(
        functools.partial(take_columns_kernel, LOCAL_WIDTH),
        out_shape=(shape, shape),
        in_specs=[IN_SMEM, IN_VMEM],
        out_specs=(IN_VMEM, IN_VMEM),
        cost_estimate=pl.CostEstimate(flops=0, bytes_accessed=2**20, transcendentals=0),
    )(spots, values)


def during(state, work):
    sent, comes = state
    done = work(lambda values: after(values, *sent))
    leaves = jax.tree.leaves(done)
    comes = lax.optimization_barrier(tuple(comes) + tuple(leaves))[: len(comes)]
    return (sent, tuple(comes)), done


def gather_near(values):
    return (values,), (shift(values, "z", 1), shift(values, "z", -1))


def gather_far(state):
    (values,), (before, following) = state
    half = values.shape[0] // 2
    across = (shift(before[:half], "z", 1), shift(following[half:], "z", -1))
    return (values, before, following), across


def gather_core(state):
    (values, before, following), (low, high) = state
    half = values.shape[0] // 2
    pieces = [values[:half], values[half:], following[:half], following[half:], low, high]
    mine = in_line(pieces + [before[:half], before[half:]])
    return (mine,), (shift(mine, "c", 1),)


def gather_value(state):
    return in_line([state[0][0], state[1][0]])


def gather_line(state, spots):
    return place([state[0][0], state[1][0]], spots, 4)


def column_spots():
    at = jnp.arange(N_BATCH)
    core, place_z = lax.axis_index("c"), lax.axis_index("z")
    return (2 * ((place_z - at // 2) % 4) + (at + core) % 2).astype(jnp.int32)


def columns_core(values):
    return (values,), (shift(values, "c", 1),)


def columns_near(state):
    both = jnp.concatenate([state[0][0], state[1][0]], axis=1)
    return (both,), tuple(shift(both, "z", step) for step in (1, 2, 3))


def columns_value(state, *awaited):
    return place_columns([state[0][0], *state[1]], column_spots(), *awaited)


def rows_core(values):
    half = values.shape[0] // 2
    given = values[half:]
    return (values, given), (shift(given, "c", 1),)


def rows_near(state):
    values, got = state[0][0], state[1][0]
    rows = values.shape[0] // 8
    pieces = []
    for step in range(4):
        spot = slice(step * rows, (step + 1) * rows)
        pieces.append(jnp.concatenate([values[spot], got[spot]], axis=1))
    return tuple(pieces), tuple(shift(pieces[step], "z", step) for step in (1, 2, 3))


def back_core(values):
    kept, given = take_columns(values, column_spots())
    return (kept, given), (shift(given, "c", 1),)


def back_near(state):
    kept, got = state[0][0], state[1][0]
    rows = kept.shape[0] // 4
    pieces = []
    for step in range(4):
        spot = slice(step * rows, (step + 1) * rows)
        pieces.append(jnp.concatenate([kept[spot], got[spot]], axis=0))
    return tuple(pieces), tuple(shift(pieces[step], "z", -step) for step in (1, 2, 3))


def back_value(state):
    pieces = [state[0][0], *state[1]]
    spots = jnp.arange(4)[:, None] + 4 * jnp.arange(2)[None, :]
    return place(pieces, spots.reshape(8).astype(jnp.int32), 2)


def add(left, right):
    return left.astype(F32) + right.astype(F32)


def sum_core(values, kind=BF16):
    core = lax.axis_index("c")
    halves = values.reshape((2, values.shape[0] // 2) + values.shape[1:])
    given = take(halves, 1 - core).astype(kind)
    return (take(halves, core), given), (shift(given, "c", 1),)


def sum_near(state):
    (kept, given), (got,) = state
    kept = add(kept, got).astype(given.dtype)
    quarter = kept.shape[0] // 2
    low, high = kept[:quarter], kept[quarter:]
    return (low, high), (pair(low, "z", neighbour_a), pair(high, "z", neighbour_b))


def sum_next(state):
    (low, high), (from_low, from_high) = state
    low, high = add(low, from_low).astype(low.dtype), add(high, from_high).astype(high.dtype)
    return (low, high), (pair(low, "z", neighbour_b), pair(high, "z", neighbour_a))


def sum_last(state):
    (low, high), (from_low, from_high) = state
    kept = jnp.concatenate([add(low, from_low), add(high, from_high)], axis=0).astype(low.dtype)
    return (kept,), (shift(kept, "c", 1),)


def sum_value(state):
    core = lax.axis_index("c")
    kept, other = state[0][0].astype(F32), state[1][0].astype(F32)
    return jnp.concatenate(
        [jnp.where(core == 0, kept, other), jnp.where(core == 0, other, kept)], axis=0
    )


def head_shards(masters, segment_ids):
    joined = jnp.concatenate([masters[0].astype(BF16), masters[1].astype(BF16)], axis=2)
    parts = joined.reshape(2, 8, 4, N_BATCH, LOCAL_WIDTH)
    parts = jnp.transpose(parts, (3, 0, 1, 2, 4)).reshape(N_BATCH, 16, 4 * LOCAL_WIDTH)
    numbers = jnp.concatenate([segment_ids, segment_ids]).astype(BF16)
    numbers = jnp.broadcast_to(numbers[None, None, :], parts.shape)
    parts = jnp.concatenate([parts, numbers], axis=1)
    moved = lax.all_to_all(parts, BATCH, split_axis=0, concat_axis=0, tiled=True)
    heads = moved[:, :16].reshape(N_BATCH, 2, 8, 4 * LOCAL_WIDTH)
    heads = jnp.transpose(heads, (1, 0, 2, 3)).reshape(2, 64, 4 * LOCAL_WIDTH)
    return heads, moved[:, 16, : segment_ids.shape[0]].reshape(-1).astype(F32)


BLOCK = 256


def masked_scores(keys, queries, key_block, query_block, key_segs, query_segs):
    scores = lax.dot_general(keys, queries, (((1,), (1,)), ((), ())), preferred_element_type=F32)
    key_pos = key_block * BLOCK + lax.broadcasted_iota(jnp.int32, (BLOCK, BLOCK), 0)
    query_pos = query_block * BLOCK + lax.broadcasted_iota(jnp.int32, (BLOCK, BLOCK), 1)
    allowed = (key_pos <= query_pos) & (key_segs == query_segs)
    return jnp.where(allowed, scores * SCORE_SCALE, NEGATIVE)


def head_columns(part, head):
    start = part * LOCAL_WIDTH + head * HDIM
    return slice(start, start + HDIM)


def attend_kernel(order, qkv, seg_row, seg_col, mixed, mixed_line, logs, keys, values_t, scores):
    block = pl.program_id(0)
    count = pl.num_programs(0)

    @pl.when(block == 0)
    def _():
        @pl.loop(0, count)
        def _(at):
            here = pl.ds(pl.multiple_of(at * BLOCK, BLOCK), BLOCK)
            rows = pl.ds(pl.multiple_of(order[at] * BLOCK, BLOCK), BLOCK)
            keys[here, :] = qkv[rows, LOCAL_WIDTH : 2 * LOCAL_WIDTH]
            values_t[:, here] = qkv[rows, 2 * LOCAL_WIDTH :].T

    here = pl.ds(pl.multiple_of(block * BLOCK, BLOCK), BLOCK)
    rows = pl.ds(pl.multiple_of(order[block] * BLOCK, BLOCK), BLOCK)
    query_segs = seg_row[:, here]
    heads = range(LOCAL_HEADS)
    queries = [qkv[rows, head_columns(0, head)] for head in heads]

    def score_step(at, tops):
        spot = pl.ds(pl.multiple_of(at * BLOCK, BLOCK), BLOCK)
        new = []
        for head in heads:
            found = masked_scores(
                keys[spot, head_columns(0, head)], queries[head], at, block, seg_col[spot, :], query_segs
            )
            scores[head, spot, :] = found
            new.append(jnp.maximum(tops[head], jnp.max(found, axis=0, keepdims=True)))
        return tuple(new)

    lowest = jnp.full((1, BLOCK), NEGATIVE, F32)
    tops = lax.fori_loop(0, block + 1, score_step, (lowest,) * LOCAL_HEADS)

    def exponent_step(at, totals):
        spot = pl.ds(pl.multiple_of(at * BLOCK, BLOCK), BLOCK)
        new = []
        for head in heads:
            exponent = jnp.exp(scores[head, spot, :] - tops[head])
            scores[head, spot, :] = exponent
            new.append(totals[head] + jnp.sum(exponent, axis=0, keepdims=True))
        return tuple(new)

    zero = jnp.zeros((1, BLOCK), F32)
    totals = lax.fori_loop(0, block + 1, exponent_step, (zero,) * LOCAL_HEADS)
    scales = [1.0 / total for total in totals]

    def value_step(at, sums):
        spot = pl.ds(pl.multiple_of(at * BLOCK, BLOCK), BLOCK)
        new = []
        for head in heads:
            probs = (scores[head, spot, :] * scales[head]).astype(BF16)
            new.append(
                sums[head]
                + jnp.dot(values_t[head_columns(0, head), spot], probs, preferred_element_type=F32)
            )
        return tuple(new)

    empty = jnp.zeros((HDIM, BLOCK), F32)
    sums = lax.fori_loop(0, block + 1, value_step, (empty,) * LOCAL_HEADS)
    result = jnp.concatenate(sums, axis=0).T.astype(BF16)
    mixed[rows, :] = result
    mixed_line[here, :] = result
    for head in heads:
        logs[head : head + 1, here] = tops[head] + jnp.log(totals[head])


def attend_back_kernel(
    order, qkv, grads, logs, seg_row, seg_col, out, out_line, keys, keys_t, values, grad_k, grad_v, probs, grad_probs
):
    block = pl.program_id(0)
    count = pl.num_programs(0)

    @pl.when(block == 0)
    def _():
        grad_k[...] = jnp.zeros_like(grad_k)
        grad_v[...] = jnp.zeros_like(grad_v)

        @pl.loop(0, count)
        def _(at):
            here = pl.ds(pl.multiple_of(at * BLOCK, BLOCK), BLOCK)
            rows = pl.ds(pl.multiple_of(order[at] * BLOCK, BLOCK), BLOCK)
            found = qkv[rows, LOCAL_WIDTH : 2 * LOCAL_WIDTH]
            keys[here, :] = found
            keys_t[:, here] = found.T
            values[here, :] = qkv[rows, 2 * LOCAL_WIDTH :]

    here = pl.ds(pl.multiple_of(block * BLOCK, BLOCK), BLOCK)
    rows = pl.ds(pl.multiple_of(order[block] * BLOCK, BLOCK), BLOCK)
    query_segs = seg_row[:, here]
    heads = range(LOCAL_HEADS)
    queries = [qkv[rows, head_columns(0, head)] for head in heads]
    grads_here = [grads[rows, head_columns(0, head)] for head in heads]
    logs_here = [logs[head : head + 1, here] for head in heads]

    def score_step(at, inners):
        spot = pl.ds(pl.multiple_of(at * BLOCK, BLOCK), BLOCK)
        new = []
        for head in heads:
            found = masked_scores(
                keys[spot, head_columns(0, head)], queries[head], at, block, seg_col[spot, :], query_segs
            )
            found = jnp.exp(found - logs_here[head])
            reached = lax.dot_general(
                values[spot, head_columns(0, head)],
                grads_here[head],
                (((1,), (1,)), ((), ())),
                preferred_element_type=F32,
            )
            probs[head, spot, :] = found
            grad_probs[head, spot, :] = reached
            new.append(inners[head] + jnp.sum(found * reached, axis=0, keepdims=True))
        return tuple(new)

    zero = jnp.zeros((1, BLOCK), F32)
    inners = lax.fori_loop(0, block + 1, score_step, (zero,) * LOCAL_HEADS)

    def grad_step(at, sums):
        spot = pl.ds(pl.multiple_of(at * BLOCK, BLOCK), BLOCK)
        new = []
        for head in heads:
            found = probs[head, spot, :]
            grad_scores = (found * (grad_probs[head, spot, :] - inners[head])).astype(BF16)
            grad_k[head, spot, :] += jnp.dot(grad_scores, queries[head], preferred_element_type=F32)
            grad_v[head, spot, :] += jnp.dot(
                found.astype(BF16), grads_here[head], preferred_element_type=F32
            )
            new.append(
                sums[head]
                + jnp.dot(keys_t[head_columns(0, head), spot], grad_scores, preferred_element_type=F32)
            )
        return tuple(new)

    empty = jnp.zeros((HDIM, BLOCK), F32)
    sums = lax.fori_loop(0, block + 1, grad_step, (empty,) * LOCAL_HEADS)
    result = (jnp.concatenate(sums, axis=0) * SCORE_SCALE).T.astype(BF16)
    out[rows, :LOCAL_WIDTH] = result
    out_line[here, :LOCAL_WIDTH] = result

    @pl.when(block == count - 1)
    def _():
        @pl.loop(0, count)
        def _(at):
            here = pl.ds(pl.multiple_of(at * BLOCK, BLOCK), BLOCK)
            rows = pl.ds(pl.multiple_of(order[at] * BLOCK, BLOCK), BLOCK)
            for head in heads:
                for part, found in ((1, grad_k[head, here, :] * SCORE_SCALE), (2, grad_v[head, here, :])):
                    out[rows, head_columns(part, head)] = found.astype(BF16)
                    out_line[here, head_columns(part, head)] = found.astype(BF16)


def skip_awaited(kernel, used, count, *refs):
    kernel(*refs[:used], *refs[used + count :])


def attend(projected, order, segments, *awaited):
    rows = projected.shape[0]
    return pl.pallas_call(
        functools.partial(skip_awaited, attend_kernel, 4, len(awaited)),
        grid=(rows // BLOCK,),
        out_shape=(
            jax.ShapeDtypeStruct((rows, LOCAL_WIDTH), BF16),
            jax.ShapeDtypeStruct((rows, LOCAL_WIDTH), BF16),
            jax.ShapeDtypeStruct((LOCAL_HEADS, rows), F32),
        ),
        in_specs=[IN_SMEM] + [IN_VMEM] * 3 + [pl.BlockSpec(memory_space=pl.ANY)] * len(awaited),
        out_specs=(IN_VMEM,) * 3,
        scratch_shapes=[
            pltpu.VMEM((rows, LOCAL_WIDTH), BF16),
            pltpu.VMEM((LOCAL_WIDTH, rows), BF16),
            pltpu.VMEM((LOCAL_HEADS, rows, BLOCK), F32),
        ],
        compiler_params=pltpu.CompilerParams(vmem_limit_bytes=40 * 2**20),
        cost_estimate=pl.CostEstimate(flops=rows, bytes_accessed=rows, transcendentals=0),
    )(order, projected, segments[None, :], segments[:, None], *awaited)


def attend_back(projected, order, segments, log_total, grad_mixed, *awaited):
    rows = projected.shape[0]
    return pl.pallas_call(
        functools.partial(skip_awaited, attend_back_kernel, 6, len(awaited)),
        grid=(rows // BLOCK,),
        out_shape=(jax.ShapeDtypeStruct((rows, 3 * LOCAL_WIDTH), BF16),) * 2,
        in_specs=[IN_SMEM] + [IN_VMEM] * 5 + [pl.BlockSpec(memory_space=pl.ANY)] * len(awaited),
        out_specs=(IN_VMEM,) * 2,
        scratch_shapes=[
            pltpu.VMEM((rows, LOCAL_WIDTH), BF16),
            pltpu.VMEM((LOCAL_WIDTH, rows), BF16),
            pltpu.VMEM((rows, LOCAL_WIDTH), BF16),
            pltpu.VMEM((LOCAL_HEADS, rows, HDIM), F32),
            pltpu.VMEM((LOCAL_HEADS, rows, HDIM), F32),
            pltpu.VMEM((LOCAL_HEADS, rows, BLOCK), F32),
            pltpu.VMEM((LOCAL_HEADS, rows, BLOCK), F32),
        ],
        compiler_params=pltpu.CompilerParams(vmem_limit_bytes=40 * 2**20),
        cost_estimate=pl.CostEstimate(flops=rows, bytes_accessed=rows, transcendentals=0),
    )(order, projected, grad_mixed, log_total, segments[None, :], segments[:, None], *awaited)


def qkv_forward(normed_all, weight_heads):
    return dot_f32("td,dc->tc", normed_all, weight_heads[:, : 3 * LOCAL_WIDTH]).astype(BF16)


def out_forward(mixed, weight_heads):
    return dot_f32("td,od->to", mixed, weight_heads[:, 3 * LOCAL_WIDTH :])


def feed_forward(normed_all, weight_up, weight_down):
    hidden = dot_f32("td,fd->tf", normed_all, weight_up)
    active = gelu_tanh(hidden).astype(BF16)
    return dot_f32("tf,fd->td", active, weight_down), hidden, active


def feed_backward(weight_up, weight_down, hidden, grad_low):
    grad_active = dot_f32("td,fd->tf", grad_low, weight_down)
    grad_hidden = jax.vjp(gelu_tanh, hidden)[1](grad_active)[0].astype(BF16)
    return grad_hidden, dot_f32("tf,fd->td", grad_hidden, weight_up)


def times(rows, gram):
    return jnp.dot(rows.astype(BF16), gram, preferred_element_type=F32)


def newton_two(rows, gram, scale):
    def polynomial(values):
        once = times(values, gram)
        return NEWTON_A * values + NEWTON_B * once + NEWTON_C * times(once, gram)

    first = polynomial(rows / scale)
    once = polynomial(times(polynomial(first), gram))
    twice = polynomial(times(polynomial(once), gram))
    return NEWTON_A * first + NEWTON_B * once + NEWTON_C * twice


def exact(left, right):
    return jnp.dot(left, right, precision=HIGHEST)


def newton_heads(block):
    gram = jnp.einsum("br,cr->bc", block, block, precision=HIGHEST)
    scale = jnp.sqrt(jnp.trace(gram)) + NEWTON_EPSILON
    gram = gram / (scale * scale)
    one = jnp.eye(HDIM, dtype=F32)
    first = NEWTON_A * one + NEWTON_B * gram + NEWTON_C * exact(gram, gram)
    gram = exact(exact(first, gram), first)
    second = NEWTON_A * one + NEWTON_B * gram + NEWTON_C * exact(gram, gram)
    return exact(exact(second, first), block / scale)


def body(
    inputs,
    cotangent,
    segment_ids,
    routed,
    qkv_master,
    out_master,
    up_master,
    down_master,
    qkv_moment,
    out_moment,
    up_moment,
    down_moment,
    router,
    router_first,
    router_second,
):
    masters = (qkv_master, out_master, up_master, down_master)
    token_count = inputs.shape[0]
    core, place_z = lax.axis_index("c"), lax.axis_index("z")
    batch_index = 2 * place_z + core
    all_tokens = jnp.arange(token_count * N_BATCH)

    at = jnp.arange(N_BATCH)
    order = (4 * ((at + core) % 2) + (at // 2 - place_z) % 4).astype(jnp.int32)
    block_of = 2 * ((at % 4 + place_z) % 4) + (at // 4 + core) % 2
    row_pos = (block_of[:, None] * token_count + jnp.arange(token_count)[None, :]).reshape(-1)
    block_of = block_of.astype(jnp.int32)
    single = jnp.zeros((1,), jnp.int32)

    normed_round = gather_near(rms_norm(inputs).astype(BF16))
    heads_local, segments_all = head_shards(masters, segment_ids)
    tied = lax.optimization_barrier((heads_local, *normed_round[1]))
    heads_local, normed_round = tied[0], (normed_round[0], tied[1:])
    heads_pair = jnp.concatenate([heads_local[1, :32], heads_local[1, 32:]], axis=1)
    wide_dense = jnp.stack([up_master[0].astype(BF16), down_master[0].astype(BF16), heads_pair])
    wide_dense = lax.all_gather(wide_dense, FSDP, axis=1, tiled=True)
    up_dense, down_dense = wide_dense[0], wide_dense[1]
    heads_pair = wide_dense[2].reshape(N_FSDP, 32, 2, 4 * LOCAL_WIDTH)
    heads_routed = jnp.transpose(heads_pair, (0, 2, 1, 3)).reshape(D, 4 * LOCAL_WIDTH)
    heads_round = gather_fsdp_first(heads_local[0])
    normed_round = gather_far(normed_round)
    tied = lax.optimization_barrier((*heads_round[1], *normed_round[1]))
    out_low = jnp.concatenate([out_master[0], out_master[1]], axis=1).astype(BF16)
    out_low = lax.all_gather(out_low, EVERY, axis=0, tiled=True)
    out_dense, out_routed = out_low[:, :D], out_low[:, D:]
    wide_routed = jnp.stack([up_master[1], down_master[1]]).astype(BF16)
    wide_routed = lax.all_gather(wide_routed, FSDP, axis=1, tiled=True)
    up_routed, down_routed = wide_routed[0], wide_routed[1]
    heads_round = gather_fsdp_second((heads_round[0], tied[:3]))
    normed_round = gather_core((normed_round[0], tied[3:]))
    heads_dense = gather_fsdp_value(heads_round)
    normed_low = gather_value(normed_round)

    chosen = routed[0]
    local_index = chosen - batch_index * token_count
    pick = (local_index[:, None] == jnp.arange(token_count)[None, :]).astype(F32)
    pick_all = (chosen[:, None] == row_pos[None, :]).astype(BF16)
    not_routed = 1.0 - jnp.max(pick, axis=0)[:, None]
    rest_grads = cotangent * not_routed
    slot_segments = jnp.sum(
        jnp.where(chosen[:, None] == all_tokens[None, :], segments_all[None, :], 0.0), axis=1
    )

    moments_heads = jnp.concatenate([qkv_moment, out_moment], axis=2).reshape(
        2, 8, 4, N_BATCH, LOCAL_WIDTH
    )
    moments_heads = jnp.transpose(moments_heads, (0, 2, 3, 1, 4))[:, :, None]
    moments_heads = jnp.broadcast_to(moments_heads, (2, 4, LOCAL_HEADS, N_BATCH, 8, LOCAL_WIDTH))
    moment_block = lax.all_to_all(
        moments_heads.reshape(128, 8, LOCAL_WIDTH), EVERY, split_axis=0, concat_axis=0, tiled=True
    ).reshape(D, LOCAL_WIDTH)
    moment_block = lax.dynamic_slice_in_dim(
        jnp.transpose(moment_block), lax.axis_index("x") % 2 * HDIM, HDIM, 0
    )

    def of_slots(values):
        return jnp.einsum("st,td->sd", pick_all, values, preferred_element_type=F32).astype(BF16)

    start_rows = jnp.einsum(
        "st,td->sd", pick, jnp.concatenate([inputs, cotangent], axis=1), precision=HIGHEST
    )
    start_round = sum_near(sum_core(after(start_rows, heads_dense), F32))
    projected = qkv_forward(normed_low, heads_dense)
    mixed_low, mixed_line, log_total = attend(
        projected, order, segments_all, *start_round[0]
    )
    mixed_slots = of_slots(mixed_low)

    slot_round = columns_core(mixed_slots)
    start_round = sum_next(
        (start_round[0], lax.optimization_barrier(start_round[1] + (mixed_slots,))[:2])
    )
    slot_round = columns_near(slot_round)
    start_round = sum_last(
        (start_round[0], lax.optimization_barrier(start_round[1] + slot_round[0])[:2])
    )
    slot_inputs = sum_value(start_round)
    slot_inputs, slot_grads = slot_inputs[:, :D], slot_inputs[:, D:]
    slot_middle = slot_inputs + dot_f32(
        "td,od->to", columns_value(slot_round), out_dense
    )
    slot_two = rms_norm(slot_middle).astype(BF16)
    slot_fed, slot_hidden, slot_active = feed_forward(slot_two, up_dense, down_dense)

    fed_round = sum_core(slot_fed)
    mixed_round = rows_core(after(mixed_low, *fed_round[0]))
    fed_round = sum_near(fed_round)
    mixed_round = rows_near(mixed_round)
    fed_round, mixed_rows = during(fed_round, lambda late: columns_value(mixed_round, moment_block))
    fed_round = sum_next(fed_round)

    def rest_forward(late):
        middle = inputs + dot_f32("td,od->to", late(mixed_rows), out_dense)
        return middle, rms_norm(middle).astype(BF16)

    fed_round, (middle, rest_two_low) = during(fed_round, rest_forward)
    fed_round = sum_last(fed_round)
    normed_two = lax.all_gather(rest_two_low, BATCH, axis=0, tiled=True)
    rest_low = lax.all_gather(
        after(rest_grads.astype(BF16), rest_two_low), BATCH, axis=0, tiled=True
    )
    slot_rows = slot_middle + sum_value(fed_round)

    slot_normed = rms_norm(slot_rows)
    slot_low = slot_normed.astype(BF16)
    r_projected = qkv_forward(slot_low, heads_routed)
    r_mixed, _, r_log_total = attend(r_projected, single, slot_segments)
    r_round = columns_core(r_mixed)
    gate_values = jnp.dot(slot_normed, router, precision=HIGHEST)
    r_round = columns_near(r_round)
    r_attended = dot_f32("td,od->to", columns_value(r_round), out_routed)
    r_middle = slot_rows + r_attended
    r_two = rms_norm(r_middle).astype(BF16)
    r_fed_part, r_hidden, r_active = feed_forward(r_two, up_routed, down_routed)

    r_round = sum_near(sum_core(r_fed_part))

    def rest_active(late):
        _, hidden, active = feed_forward(late(normed_two), up_dense, down_dense)
        return hidden, active

    r_round, (feed_hidden, feed_active) = during(r_round, rest_active)
    r_round = sum_last(sum_next(r_round))
    routed_branch = r_attended + sum_value(r_round)

    branch_grads = gate_values[:, None] * slot_grads
    branch_low = branch_grads.astype(BF16)
    r_grad_hidden, r_grad_two = feed_backward(up_routed, down_routed, r_hidden, branch_low)

    r_round = sum_near(sum_core(r_grad_two))

    def rest_back(late):
        grad_active = dot_f32("td,fd->tf", late(rest_low), down_dense)
        return jax.vjp(gelu_tanh, feed_hidden)[1](grad_active)[0].astype(BF16)

    r_round, rest_hidden = during(r_round, rest_back)
    r_round = sum_next(r_round)
    r_round, rest_two = during(r_round, lambda late: dot_f32("tf,fd->td", late(rest_hidden), up_dense))
    rest_two = lax.psum_scatter(rest_two.astype(BF16), BATCH, scatter_dimension=0, tiled=True)
    r_round = sum_last(r_round)

    def routed_weights(late):
        return (
            dot_f32("tf,td->fd", late(r_grad_hidden), r_two),
            dot_f32("tf,td->fd", r_active, late(branch_low)),
            jnp.sum(slot_grads * routed_branch, axis=1),
        )

    r_round, (r_grad_up, r_grad_down, gate_grads) = during(r_round, routed_weights)
    r_grad_mid = norm_back(r_middle, sum_value(r_round))
    r_grad_low = (r_grad_mid + branch_grads).astype(BF16)

    def out_back(grad_low, weight_heads):
        return dot_f32("to,od->td", grad_low, weight_heads[:, 3 * LOCAL_WIDTH :]).astype(BF16)

    r_grad_projected, _ = attend_back(
        r_projected, single, slot_segments, r_log_total, out_back(r_grad_low, heads_routed)
    )
    r_round = sum_core(dot_f32("tc,dc->td", r_grad_projected, heads_routed[:, : 3 * LOCAL_WIDTH]))
    r_round = sum_near(r_round)
    r_round, rest_up = during(
        r_round, lambda late: dot_f32("tf,td->fd", late(rest_hidden), normed_two)
    )
    r_round = sum_next(r_round)
    r_round, rest_down = during(
        r_round, lambda late: dot_f32("tf,td->fd", feed_active, late(rest_low))
    )
    r_round = sum_last(r_round)
    r_grad_normed = sum_value(r_round)
    slot_out_grads = (
        slot_grads
        + r_grad_mid
        + norm_back(slot_rows, r_grad_normed + gate_grads[:, None] * router[None, :])
    )

    slot_out_low = slot_out_grads.astype(BF16)
    slot_grad_hidden, slot_grad_two = feed_backward(up_dense, down_dense, slot_hidden, slot_out_low)
    slot_round = sum_near(sum_core(slot_grad_two))
    def routed_heads(late):
        return (
            dot_f32("tc,td->cd", late(r_grad_projected), slot_low),
            dot_f32("td,to->do", r_mixed, late(r_grad_low)),
        )

    slot_round, (r_grad_qkv, r_grad_out) = during(slot_round, routed_heads)
    slot_round = sum_next(slot_round)
    slot_round, fed_line = during(
        slot_round, lambda late: dot_f32("tf,fd->td", late(feed_active), down_dense)
    )
    slot_round = sum_last(slot_round)
    slot_mid = slot_out_grads + norm_back(slot_middle, sum_value(slot_round))
    slot_mid_low = slot_mid.astype(BF16)
    slot_mixed = out_back(slot_mid_low, heads_dense)
    grad_up = rest_up + dot_f32("tf,td->fd", slot_grad_hidden, slot_two)
    grad_down = rest_down + dot_f32("tf,td->fd", slot_active, slot_out_low)
    wide_round = scatter_fsdp_first(grad_up, r_grad_up, grad_down, r_grad_down)

    rest_two = after(rest_two, *wide_round[0], slot_mixed)
    rest_mid = rest_grads + norm_back(middle, rest_two.astype(F32))
    rest_mid_low = rest_mid.astype(BF16)
    rest_mixed = dot_f32("to,od->td", rest_mid_low, out_dense).astype(BF16)
    rest_mid_all = lax.all_gather(rest_mid_low, BATCH, axis=0, tiled=True)
    rest_mixed = back_value(back_near(back_core(rest_mixed)))
    grad_mixed = (
        rest_mixed.astype(F32)
        + jnp.einsum("st,sd->td", pick_all, slot_mixed, preferred_element_type=F32)
    ).astype(BF16)
    grad_mixed = after(grad_mixed, *wide_round[0])
    fed_rows = lax.psum_scatter(after(fed_line, grad_mixed), BATCH, scatter_dimension=0, tiled=True)
    grad_projected, grad_projected_line = attend_back(projected, order, segments_all, log_total, grad_mixed)

    wide_round = (
        wide_round[0],
        lax.optimization_barrier(wide_round[1] + (grad_projected,))[:3],
    )
    wide_round = scatter_fsdp_second(wide_round)

    def dense_weights(late):
        grads = late(grad_projected)
        grad_qkv = dot_f32("tc,td->cd", grads, normed_low)
        grad_out = dot_f32("td,to->do", mixed_line, rest_mid_all) + dot_f32(
            "td,to->do", mixed_slots, slot_mid_low
        )
        return grad_qkv, grad_out

    wide_round, (grad_qkv, grad_out) = during(wide_round, dense_weights)

    block_parts = jnp.concatenate([grad_qkv, grad_out, r_grad_qkv, r_grad_out], axis=0).astype(BF16)
    router_grad = jnp.dot(gate_grads, slot_normed, precision=HIGHEST)
    router_high = router_grad.astype(BF16)
    router_low = (router_grad - router_high.astype(F32)).astype(BF16)
    router_rows = jnp.concatenate(
        [router_high[None, :], router_low[None, :], jnp.zeros((14, D), BF16)], axis=0
    )
    block_parts = jnp.concatenate(
        [block_parts.reshape(16, HDIM, D), jnp.broadcast_to(router_rows[None], (16, 16, D))], axis=1
    )
    heads_round = scatter_fsdp_first(block_parts.reshape(-1, D))

    wide_grads = turn_total(wide_round).reshape(4, 32, D)
    new_up_moment = MOMENTUM * up_moment + wide_grads[:2]
    new_down_moment = MOMENTUM * down_moment + wide_grads[2:]
    wide_own = after(jnp.concatenate([new_up_moment, new_down_moment], axis=0), *heads_round[0])
    wide_round = exchange_near(wide_own)
    wide_round, grad_normed = during(
        wide_round,
        lambda late: dot_f32("tc,dc->td", late(grad_projected_line), heads_dense[:, : 3 * LOCAL_WIDTH]),
    )
    wide_rows = exchange_value(wide_round)
    rows_low = wide_rows.astype(BF16)
    rows_both = jnp.concatenate([rows_low, shift(rows_low, "c", 1)], axis=0)
    heads_round = (heads_round[0], lax.optimization_barrier(heads_round[1] + (rows_both,))[:3])
    heads_round = turn_parts(turn_total(heads_round), True)
    rows_both = after(rows_both, *heads_round[0])
    grad_normed = lax.psum_scatter(
        after(grad_normed, rows_both), BATCH, scatter_dimension=0, tiled=True
    )
    own_columns = lax.dynamic_slice_in_dim(rows_both, core * (D // 2), D // 2, 1)
    gram_part = dot_f32("rb,rc->bc", own_columns, rows_both)

    def heads_step(late):
        grads = turn_total(heads_round)
        new_block = MOMENTUM * moment_block + late(grads)[:HDIM]
        ortho_block = newton_heads(new_block)
        returned = jnp.transpose(jnp.concatenate([new_block, ortho_block], axis=0))
        return returned.reshape(128, 8, 2 * HDIM), grads[HDIM] + grads[HDIM + 1]

    gram_round = turn_second(turn_first(gram_part))
    gram_round, (returned, router_total) = during(gram_round, heads_step)
    gram_round = turn_third(gram_round)
    returned = lax.all_to_all(returned, EVERY, split_axis=0, concat_axis=0, tiled=True)
    gram_round = turn_fourth(gram_round)
    gram_round, mixed = during(
        gram_round,
        lambda late: middle
        + late(fed_rows)
        + jnp.einsum("st,sd->td", pick, gate_values[:, None] * routed_branch, precision=HIGHEST),
    )
    gram_half = turn_value(gram_round)
    gram_other = shift(gram_half, "c", 1)
    wide_gram = jnp.concatenate(
        [jnp.where(core == 0, gram_half, gram_other), jnp.where(core == 0, gram_other, gram_half)],
        axis=0,
    )
    wide_scale = jnp.sqrt(jnp.trace(wide_gram.astype(F32))) + NEWTON_EPSILON
    wide_gram = (wide_gram.astype(F32) / (wide_scale * wide_scale)).astype(BF16)
    wide_ortho = newton_two(wide_rows, wide_gram, wide_scale).reshape(4, 32, D)
    wide_round = exchange_near(wide_ortho)

    def token_step(late):
        grad_mid = rest_mid + jnp.einsum("st,sd->td", pick, slot_mid, precision=HIGHEST)
        grad_inputs = grad_mid + norm_back(inputs, late(grad_normed))
        return grad_inputs

    wide_round, grad_inputs = during(wide_round, token_step)
    wide_ortho = exchange_value(wide_round).reshape(4, 32, D)

    returned = returned.reshape(2, 4, LOCAL_HEADS, N_BATCH, 8, 2, HDIM)
    returned = jnp.transpose(returned, (5, 0, 4, 1, 3, 2, 6)).reshape(2, 2, 8, 4 * D)
    new_moments = (returned[0, :, :, : 3 * D], returned[0, :, :, 3 * D :], new_up_moment, new_down_moment)
    orthos = (returned[1, :, :, : 3 * D], returned[1, :, :, 3 * D :], wide_ortho[:2], wide_ortho[2:])

    widths = (HDIM, HDIM, D, D)
    full_rows = (D, D, FF, FF)
    new_masters = []
    for index_type in range(4):
        rate = STEP_RATES[index_type]
        factor = 0.2 * math.sqrt(max(full_rows[index_type], widths[index_type]))
        new_masters.append(
            masters[index_type] * (1.0 - rate * WEIGHT_DECAY) - rate * factor * orthos[index_type]
        )
    first_new = FIRST_DECAY * router_first + (1.0 - FIRST_DECAY) * router_total
    second_new = SECOND_DECAY * router_second + (1.0 - SECOND_DECAY) * router_total * router_total
    corrected_first = first_new / (1.0 - FIRST_DECAY**STEP)
    corrected_second = second_new / (1.0 - SECOND_DECAY**STEP)
    router_new = router * (1.0 - ADAM_RATE * WEIGHT_DECAY) - ADAM_RATE * corrected_first / (
        jnp.sqrt(corrected_second) + ADAM_EPSILON
    )
    return (
        (mixed, grad_inputs)
        + new_moments
        + tuple(new_masters)
        + tuple(master.astype(BF16) for master in new_masters)
        + (router_new, first_new, second_new)
    )


def solution(mesh):
    fine = Mesh(mesh.devices.reshape(4, 4, 4, 2), EVERY)
    tokens = P(EVERY, None)
    weights = P(None, EVERY, None)
    return jax.shard_map(
        body,
        mesh=fine,
        in_specs=(tokens, tokens, P(EVERY), P(FSDP, None)) + (weights,) * 8 + (P(),) * 3,
        out_specs=(tokens, tokens) + (weights,) * 12 + (P(),) * 3,
        check_vma=False,
    )
```

```python
import functools
import math

import jax
import jax.numpy as jnp
from jax import lax
from jax.experimental import pallas as pl
from jax.experimental.pallas import tpu as pltpu
from jax.sharding import Mesh
from jax.sharding import PartitionSpec as P

D = 1024
HEADS = 16
HDIM = 64
FF = 4096
STEP = 8
N_FSDP = 16
N_BATCH = 8
LOCAL_HEADS = HEADS // N_BATCH
LOCAL_WIDTH = LOCAL_HEADS * HDIM
K_ROUTE = 256

EPSILON = 1e-05
SCORE_SCALE = 0.125
NEGATIVE = -1e30
MOMENTUM = 0.95
WEIGHT_DECAY = 0.01
STEP_RATES = (0.15, 1.0, 0.15, 0.15)
NEWTON_A = 3.4445
NEWTON_B = -4.775
NEWTON_C = 2.0315
NEWTON_EPSILON = 1e-07
ADAM_RATE = 0.03
FIRST_DECAY = 0.9
SECOND_DECAY = 0.95
ADAM_EPSILON = 1e-08
HIGHEST = lax.Precision.HIGHEST
F32 = jnp.float32
BF16 = jnp.bfloat16

FSDP = ("y", "x")
BATCH = ("z", "c")
EVERY = ("y", "x", "z", "c")

IN_VMEM = pl.BlockSpec(memory_space=pltpu.VMEM)
IN_SMEM = pl.BlockSpec(memory_space=pltpu.SMEM)


def rms_norm(values):
    return values * lax.rsqrt(jnp.mean(values * values, axis=-1, keepdims=True) + EPSILON)


def gelu_tanh(values):
    return jax.nn.gelu(values, approximate=True)


def norm_back(values, grad_normed):
    pull_back = jax.vjp(rms_norm, values)[1]
    return pull_back(grad_normed)[0]


def dot_f32(pattern, left, right):
    return jnp.einsum(pattern, left, right, preferred_element_type=F32)


def shift(values, axis, step):
    size = 2 if axis == "c" else 4
    return lax.ppermute(values, axis, [(i, (i + step) % size) for i in range(size)])


def pair(values, axis, partner):
    return lax.ppermute(values, axis, [(i, partner(i)) for i in range(4)])


def neighbour_a(i):
    return i ^ 1


def neighbour_b(i):
    return 3 - i


def after(values, *others):
    return lax.optimization_barrier((values,) + others)[0]


def take(values, index):
    return lax.dynamic_index_in_dim(values, index, 0, keepdims=False)


def put(values, piece, index):
    return lax.dynamic_update_index_in_dim(values, piece, index, 0)


def turn(values, step, last=False):
    pairs = []
    for y in range(4):
        for x in range(4):
            for core in range(2):
                along_x = (core == 0) != last
                to_y, to_x = (y, (x + step) % 4) if along_x else ((y + step) % 4, x)
                pairs.append(((y * 4 + x) * 2 + core, (to_y * 4 + to_x) * 2 + core))
    return lax.ppermute(values, ("y", "x", "c"), pairs)


def turn_place(last=False):
    along_x = (lax.axis_index("c") == 0) != last
    return jnp.where(along_x, lax.axis_index("x"), lax.axis_index("y"))


def copy_rows(target, start, source, first, rows):
    step = math.gcd(rows, 64)

    @pl.loop(0, rows // step)
    def _(at):
        here = pl.ds(pl.multiple_of(first + at * step, step), step)
        there = pl.ds(pl.multiple_of(start + at * step, step), step)
        target[there, :] = source[here, :].astype(target.dtype)


def place_kernel(piece_count, sub_count, spots, *refs):
    pieces, whole = refs[:piece_count], refs[piece_count]
    rows = pieces[0].shape[0] // sub_count
    for p in range(piece_count):
        for s in range(sub_count):
            start = pl.multiple_of(spots[p * sub_count + s] * rows, rows)
            copy_rows(whole, start, pieces[p], s * rows, rows)


def place(pieces, spots, sub_count=1):
    rows = len(pieces) * pieces[0].shape[0]
    shape = (rows,) + pieces[0].shape[1:]
    size = math.prod(shape) * pieces[0].dtype.itemsize
    return pl.pallas_call(
        functools.partial(place_kernel, len(pieces), sub_count),
        out_shape=jax.ShapeDtypeStruct(shape, pieces[0].dtype),
        in_specs=[IN_SMEM] + [IN_VMEM] * len(pieces),
        out_specs=IN_VMEM,
        compiler_params=pltpu.CompilerParams(vmem_limit_bytes=40 * 2**20),
        cost_estimate=pl.CostEstimate(flops=0, bytes_accessed=2 * size, transcendentals=0),
    )(spots, *pieces)


def split_kernel(rows, count, spots, *refs):
    values, outs = refs[:count], refs[count:]
    for step in range(4):
        for i in range(4):
            first = pl.multiple_of(spots[4 * step + i] * rows, rows)
            for at, source in enumerate(values):
                copy_rows(outs[step], (count * i + at) * rows, source, first, rows)


def split(values, spots):
    count = len(values)
    rows = values[0].shape[0] // 16
    shape = jax.ShapeDtypeStruct((4 * count * rows, values[0].shape[1]), BF16)
    return pl.pallas_call(
        functools.partial(split_kernel, rows, count),
        out_shape=(shape,) * 4,
        in_specs=[IN_SMEM] + [IN_VMEM] * count,
        out_specs=(IN_VMEM,) * 4,
        compiler_params=pltpu.CompilerParams(vmem_limit_bytes=40 * 2**20),
        cost_estimate=pl.CostEstimate(flops=0, bytes_accessed=2**22, transcendentals=0),
    )(spots, *values)


def in_line(pieces):
    return place(pieces, jnp.arange(len(pieces), dtype=jnp.int32))


def gather_fsdp_first(values):
    return (values,), tuple(turn(values, step) for step in (1, 2, 3))


def gather_fsdp_second(state):
    line = in_line([state[0][0], *state[1]])
    return (line,), tuple(turn(line, step, True) for step in (1, 2, 3))


def gather_fsdp_value(state):
    core = lax.axis_index("c")
    mine, far = turn_place(), turn_place(True)
    step = jnp.arange(4)
    first, second = (mine - step[None, :]) % 4, (far - step[:, None]) % 4
    spots = jnp.where(core == 0, second * 4 + first, first * 4 + second)
    return place([state[0][0], *state[1]], spots.reshape(16).astype(jnp.int32), 4)


def turn_parts(parts, last=False):
    me = turn_place(last)
    parts = parts.reshape((4, -1) + parts.shape[1:])
    sent = tuple(take(parts, (me + step) % 4).astype(BF16) for step in (1, 2, 3))
    own = take(parts, me).astype(F32)
    return (own,) + sent, tuple(turn(sent[i], i + 1, last) for i in range(3))


def turn_total(state):
    total = state[0][0].astype(F32)
    for piece in state[1]:
        total = total + piece.astype(F32)
    return total


def scatter_fsdp_first(*values):
    core = lax.axis_index("c")
    me = turn_place()
    step, other = jnp.arange(4)[:, None], jnp.arange(4)[None, :]
    spot = (me + step) % 4
    spots = jnp.where(core == 0, other * 4 + spot, spot * 4 + other)
    parts = split(values, spots.reshape(16).astype(jnp.int32))
    return tuple(parts), tuple(turn(parts[step], step) for step in (1, 2, 3))


def scatter_fsdp_second(state):
    return turn_parts(turn_total(state), True)


def exchange_near(values):
    place_z = lax.axis_index("z")
    pieces = tuple(take(values, (place_z + step) % 4) for step in range(4))
    return pieces, tuple(shift(pieces[step], "z", step) for step in (1, 2, 3))


def exchange_value(state):
    spots = (lax.axis_index("z") - jnp.arange(4)) % 4
    return place([state[0][0], *state[1]], spots.astype(jnp.int32))


def turn_first(values):
    return turn_parts(values)


def turn_second(state):
    return turn_parts(turn_total(state), True)


def turn_third(state):
    total = turn_total(state).astype(BF16)
    return (total,), tuple(turn(total, step, True) for step in (1, 2, 3))


def turn_fourth(state):
    spots = (turn_place(True) - jnp.arange(4)) % 4
    line = place([state[0][0], *state[1]], spots.astype(jnp.int32))
    return (line,), tuple(turn(line, step) for step in (1, 2, 3))


def turn_value(state):
    spots = (turn_place() - jnp.arange(4)) % 4
    return place([state[0][0], *state[1]], spots.astype(jnp.int32))


def place_columns_kernel(width, count, spots, *refs):
    pieces, whole = refs[:count], refs[-1]
    for p, piece in enumerate(pieces):
        for s in range(piece.shape[1] // width):
            start = pl.multiple_of(spots[p * (piece.shape[1] // width) + s] * width, width)
            whole[:, pl.ds(start, width)] = piece[:, s * width : (s + 1) * width]


def place_columns(pieces, spots, *awaited):
    rows, width = pieces[0].shape
    return pl.pallas_call(
        functools.partial(place_columns_kernel, LOCAL_WIDTH, len(pieces)),
        out_shape=jax.ShapeDtypeStruct((rows, width * len(pieces)), pieces[0].dtype),
        in_specs=[IN_SMEM]
        + [IN_VMEM] * len(pieces)
        + [pl.BlockSpec(memory_space=pl.ANY)] * len(awaited),
        out_specs=IN_VMEM,
        cost_estimate=pl.CostEstimate(flops=0, bytes_accessed=2**20, transcendentals=0),
    )(spots, *pieces, *awaited)


def take_columns_kernel(width, spots, values, kept, given):
    rows = values.shape[0]
    for step in range(4):
        for i, out in enumerate((kept, given)):
            start = pl.multiple_of(spots[2 * step + i] * width, width)
            out[step * rows : (step + 1) * rows, :] = values[:, pl.ds(start, width)]


def take_columns(values, spots):
    shape = jax.ShapeDtypeStruct((4 * values.shape[0], LOCAL_WIDTH), values.dtype)
    return pl.pallas_call(
        functools.partial(take_columns_kernel, LOCAL_WIDTH),
        out_shape=(shape, shape),
        in_specs=[IN_SMEM, IN_VMEM],
        out_specs=(IN_VMEM, IN_VMEM),
        cost_estimate=pl.CostEstimate(flops=0, bytes_accessed=2**20, transcendentals=0),
    )(spots, values)


def during(state, work):
    sent, comes = state
    done = work(lambda values: after(values, *sent))
    leaves = jax.tree.leaves(done)
    comes = lax.optimization_barrier(tuple(comes) + tuple(leaves))[: len(comes)]
    return (sent, tuple(comes)), done


def gather_near(values):
    return (values,), (shift(values, "z", 1), shift(values, "z", -1))


def gather_far(state):
    (values,), (before, following) = state
    half = values.shape[0] // 2
    across = (shift(before[:half], "z", 1), shift(following[half:], "z", -1))
    return (values, before, following), across


def gather_core(state):
    (values, before, following), (low, high) = state
    half = values.shape[0] // 2
    pieces = [values[:half], values[half:], following[:half], following[half:], low, high]
    mine = in_line(pieces + [before[:half], before[half:]])
    return (mine,), (shift(mine, "c", 1),)


def gather_value(state):
    return in_line([state[0][0], state[1][0]])


def gather_line(state, spots):
    return place([state[0][0], state[1][0]], spots, 4)


def column_spots():
    at = jnp.arange(N_BATCH)
    core, place_z = lax.axis_index("c"), lax.axis_index("z")
    return (2 * ((place_z - at // 2) % 4) + (at + core) % 2).astype(jnp.int32)


def columns_core(values):
    return (values,), (shift(values, "c", 1),)


def columns_near(state):
    both = jnp.concatenate([state[0][0], state[1][0]], axis=1)
    return (both,), tuple(shift(both, "z", step) for step in (1, 2, 3))


def columns_value(state, *awaited):
    return place_columns([state[0][0], *state[1]], column_spots(), *awaited)


def rows_core(values):
    half = values.shape[0] // 2
    given = values[half:]
    return (values, given), (shift(given, "c", 1),)


def rows_near(state):
    values, got = state[0][0], state[1][0]
    rows = values.shape[0] // 8
    pieces = []
    for step in range(4):
        spot = slice(step * rows, (step + 1) * rows)
        pieces.append(jnp.concatenate([values[spot], got[spot]], axis=1))
    return tuple(pieces), tuple(shift(pieces[step], "z", step) for step in (1, 2, 3))


def back_core(values):
    kept, given = take_columns(values, column_spots())
    return (kept, given), (shift(given, "c", 1),)


def back_near(state):
    kept, got = state[0][0], state[1][0]
    rows = kept.shape[0] // 4
    pieces = []
    for step in range(4):
        spot = slice(step * rows, (step + 1) * rows)
        pieces.append(jnp.concatenate([kept[spot], got[spot]], axis=0))
    return tuple(pieces), tuple(shift(pieces[step], "z", -step) for step in (1, 2, 3))


def back_value(state):
    pieces = [state[0][0], *state[1]]
    spots = jnp.arange(4)[:, None] + 4 * jnp.arange(2)[None, :]
    return place(pieces, spots.reshape(8).astype(jnp.int32), 2)


def add(left, right):
    return left.astype(F32) + right.astype(F32)


def sum_core(values, kind=BF16):
    core = lax.axis_index("c")
    halves = values.reshape((2, values.shape[0] // 2) + values.shape[1:])
    given = take(halves, 1 - core).astype(kind)
    return (take(halves, core), given), (shift(given, "c", 1),)


def sum_near(state):
    (kept, given), (got,) = state
    kept = add(kept, got).astype(given.dtype)
    quarter = kept.shape[0] // 2
    low, high = kept[:quarter], kept[quarter:]
    return (low, high), (pair(low, "z", neighbour_a), pair(high, "z", neighbour_b))


def sum_next(state):
    (low, high), (from_low, from_high) = state
    low, high = add(low, from_low).astype(low.dtype), add(high, from_high).astype(high.dtype)
    return (low, high), (pair(low, "z", neighbour_b), pair(high, "z", neighbour_a))


def sum_last(state):
    (low, high), (from_low, from_high) = state
    kept = jnp.concatenate([add(low, from_low), add(high, from_high)], axis=0).astype(low.dtype)
    return (kept,), (shift(kept, "c", 1),)


def sum_value(state):
    core = lax.axis_index("c")
    kept, other = state[0][0].astype(F32), state[1][0].astype(F32)
    return jnp.concatenate(
        [jnp.where(core == 0, kept, other), jnp.where(core == 0, other, kept)], axis=0
    )


def head_shards(masters, segment_ids):
    joined = jnp.concatenate([masters[0].astype(BF16), masters[1].astype(BF16)], axis=2)
    parts = joined.reshape(2, 8, 4, N_BATCH, LOCAL_WIDTH)
    parts = jnp.transpose(parts, (3, 0, 1, 2, 4)).reshape(N_BATCH, 16, 4 * LOCAL_WIDTH)
    numbers = jnp.concatenate([segment_ids, segment_ids]).astype(BF16)
    numbers = jnp.broadcast_to(numbers[None, None, :], parts.shape)
    parts = jnp.concatenate([parts, numbers], axis=1)
    moved = lax.all_to_all(parts, BATCH, split_axis=0, concat_axis=0, tiled=True)
    heads = moved[:, :16].reshape(N_BATCH, 2, 8, 4 * LOCAL_WIDTH)
    heads = jnp.transpose(heads, (1, 0, 2, 3)).reshape(2, 64, 4 * LOCAL_WIDTH)
    return heads, moved[:, 16, : segment_ids.shape[0]].reshape(-1).astype(F32)


BLOCK = 256


def masked_scores(keys, queries, key_block, query_block, key_segs, query_segs):
    scores = lax.dot_general(keys, queries, (((1,), (1,)), ((), ())), preferred_element_type=F32)
    key_pos = key_block * BLOCK + lax.broadcasted_iota(jnp.int32, (BLOCK, BLOCK), 0)
    query_pos = query_block * BLOCK + lax.broadcasted_iota(jnp.int32, (BLOCK, BLOCK), 1)
    allowed = (key_pos <= query_pos) & (key_segs == query_segs)
    return jnp.where(allowed, scores * SCORE_SCALE, NEGATIVE)


def head_columns(part, head):
    start = part * LOCAL_WIDTH + head * HDIM
    return slice(start, start + HDIM)


def attend_kernel(order, qkv, seg_row, seg_col, mixed, mixed_line, logs, keys, values_t, scores):
    block = pl.program_id(0)
    count = pl.num_programs(0)

    @pl.when(block == 0)
    def _():
        @pl.loop(0, count)
        def _(at):
            here = pl.ds(pl.multiple_of(at * BLOCK, BLOCK), BLOCK)
            rows = pl.ds(pl.multiple_of(order[at] * BLOCK, BLOCK), BLOCK)
            keys[here, :] = qkv[rows, LOCAL_WIDTH : 2 * LOCAL_WIDTH]
            values_t[:, here] = qkv[rows, 2 * LOCAL_WIDTH :].T

    here = pl.ds(pl.multiple_of(block * BLOCK, BLOCK), BLOCK)
    rows = pl.ds(pl.multiple_of(order[block] * BLOCK, BLOCK), BLOCK)
    query_segs = seg_row[:, here]
    heads = range(LOCAL_HEADS)
    queries = [qkv[rows, head_columns(0, head)] for head in heads]

    def score_step(at, tops):
        spot = pl.ds(pl.multiple_of(at * BLOCK, BLOCK), BLOCK)
        new = []
        for head in heads:
            found = masked_scores(
                keys[spot, head_columns(0, head)], queries[head], at, block, seg_col[spot, :], query_segs
            )
            scores[head, spot, :] = found
            new.append(jnp.maximum(tops[head], jnp.max(found, axis=0, keepdims=True)))
        return tuple(new)

    lowest = jnp.full((1, BLOCK), NEGATIVE, F32)
    tops = lax.fori_loop(0, block + 1, score_step, (lowest,) * LOCAL_HEADS)

    def exponent_step(at, totals):
        spot = pl.ds(pl.multiple_of(at * BLOCK, BLOCK), BLOCK)
        new = []
        for head in heads:
            exponent = jnp.exp(scores[head, spot, :] - tops[head])
            scores[head, spot, :] = exponent
            new.append(totals[head] + jnp.sum(exponent, axis=0, keepdims=True))
        return tuple(new)

    zero = jnp.zeros((1, BLOCK), F32)
    totals = lax.fori_loop(0, block + 1, exponent_step, (zero,) * LOCAL_HEADS)
    scales = [1.0 / total for total in totals]

    def value_step(at, sums):
        spot = pl.ds(pl.multiple_of(at * BLOCK, BLOCK), BLOCK)
        new = []
        for head in heads:
            probs = (scores[head, spot, :] * scales[head]).astype(BF16)
            new.append(
                sums[head]
                + jnp.dot(values_t[head_columns(0, head), spot], probs, preferred_element_type=F32)
            )
        return tuple(new)

    empty = jnp.zeros((HDIM, BLOCK), F32)
    sums = lax.fori_loop(0, block + 1, value_step, (empty,) * LOCAL_HEADS)
    result = jnp.concatenate(sums, axis=0).T.astype(BF16)
    mixed[rows, :] = result
    mixed_line[here, :] = result
    for head in heads:
        logs[head : head + 1, here] = tops[head] + jnp.log(totals[head])


def attend_back_kernel(
    order, qkv, grads, logs, seg_row, seg_col, out, out_line, keys, keys_t, values, grad_k, grad_v, probs, grad_probs
):
    block = pl.program_id(0)
    count = pl.num_programs(0)

    @pl.when(block == 0)
    def _():
        grad_k[...] = jnp.zeros_like(grad_k)
        grad_v[...] = jnp.zeros_like(grad_v)

        @pl.loop(0, count)
        def _(at):
            here = pl.ds(pl.multiple_of(at * BLOCK, BLOCK), BLOCK)
            rows = pl.ds(pl.multiple_of(order[at] * BLOCK, BLOCK), BLOCK)
            found = qkv[rows, LOCAL_WIDTH : 2 * LOCAL_WIDTH]
            keys[here, :] = found
            keys_t[:, here] = found.T
            values[here, :] = qkv[rows, 2 * LOCAL_WIDTH :]

    here = pl.ds(pl.multiple_of(block * BLOCK, BLOCK), BLOCK)
    rows = pl.ds(pl.multiple_of(order[block] * BLOCK, BLOCK), BLOCK)
    query_segs = seg_row[:, here]
    heads = range(LOCAL_HEADS)
    queries = [qkv[rows, head_columns(0, head)] for head in heads]
    grads_here = [grads[rows, head_columns(0, head)] for head in heads]
    logs_here = [logs[head : head + 1, here] for head in heads]

    def score_step(at, inners):
        spot = pl.ds(pl.multiple_of(at * BLOCK, BLOCK), BLOCK)
        new = []
        for head in heads:
            found = masked_scores(
                keys[spot, head_columns(0, head)], queries[head], at, block, seg_col[spot, :], query_segs
            )
            found = jnp.exp(found - logs_here[head])
            reached = lax.dot_general(
                values[spot, head_columns(0, head)],
                grads_here[head],
                (((1,), (1,)), ((), ())),
                preferred_element_type=F32,
            )
            probs[head, spot, :] = found
            grad_probs[head, spot, :] = reached
            new.append(inners[head] + jnp.sum(found * reached, axis=0, keepdims=True))
        return tuple(new)

    zero = jnp.zeros((1, BLOCK), F32)
    inners = lax.fori_loop(0, block + 1, score_step, (zero,) * LOCAL_HEADS)

    def grad_step(at, sums):
        spot = pl.ds(pl.multiple_of(at * BLOCK, BLOCK), BLOCK)
        new = []
        for head in heads:
            found = probs[head, spot, :]
            grad_scores = (found * (grad_probs[head, spot, :] - inners[head])).astype(BF16)
            grad_k[head, spot, :] += jnp.dot(grad_scores, queries[head], preferred_element_type=F32)
            grad_v[head, spot, :] += jnp.dot(
                found.astype(BF16), grads_here[head], preferred_element_type=F32
            )
            new.append(
                sums[head]
                + jnp.dot(keys_t[head_columns(0, head), spot], grad_scores, preferred_element_type=F32)
            )
        return tuple(new)

    empty = jnp.zeros((HDIM, BLOCK), F32)
    sums = lax.fori_loop(0, block + 1, grad_step, (empty,) * LOCAL_HEADS)
    result = (jnp.concatenate(sums, axis=0) * SCORE_SCALE).T.astype(BF16)
    out[rows, :LOCAL_WIDTH] = result
    out_line[here, :LOCAL_WIDTH] = result

    @pl.when(block == count - 1)
    def _():
        @pl.loop(0, count)
        def _(at):
            here = pl.ds(pl.multiple_of(at * BLOCK, BLOCK), BLOCK)
            rows = pl.ds(pl.multiple_of(order[at] * BLOCK, BLOCK), BLOCK)
            for head in heads:
                for part, found in ((1, grad_k[head, here, :] * SCORE_SCALE), (2, grad_v[head, here, :])):
                    out[rows, head_columns(part, head)] = found.astype(BF16)
                    out_line[here, head_columns(part, head)] = found.astype(BF16)


def skip_awaited(kernel, used, count, *refs):
    kernel(*refs[:used], *refs[used + count :])


def attend(projected, order, segments, *awaited):
    rows = projected.shape[0]
    return pl.pallas_call(
        functools.partial(skip_awaited, attend_kernel, 4, len(awaited)),
        grid=(rows // BLOCK,),
        out_shape=(
            jax.ShapeDtypeStruct((rows, LOCAL_WIDTH), BF16),
            jax.ShapeDtypeStruct((rows, LOCAL_WIDTH), BF16),
            jax.ShapeDtypeStruct((LOCAL_HEADS, rows), F32),
        ),
        in_specs=[IN_SMEM] + [IN_VMEM] * 3 + [pl.BlockSpec(memory_space=pl.ANY)] * len(awaited),
        out_specs=(IN_VMEM,) * 3,
        scratch_shapes=[
            pltpu.VMEM((rows, LOCAL_WIDTH), BF16),
            pltpu.VMEM((LOCAL_WIDTH, rows), BF16),
            pltpu.VMEM((LOCAL_HEADS, rows, BLOCK), F32),
        ],
        compiler_params=pltpu.CompilerParams(vmem_limit_bytes=40 * 2**20),
        cost_estimate=pl.CostEstimate(flops=rows, bytes_accessed=rows, transcendentals=0),
    )(order, projected, segments[None, :], segments[:, None], *awaited)


def attend_back(projected, order, segments, log_total, grad_mixed, *awaited):
    rows = projected.shape[0]
    return pl.pallas_call(
        functools.partial(skip_awaited, attend_back_kernel, 6, len(awaited)),
        grid=(rows // BLOCK,),
        out_shape=(jax.ShapeDtypeStruct((rows, 3 * LOCAL_WIDTH), BF16),) * 2,
        in_specs=[IN_SMEM] + [IN_VMEM] * 5 + [pl.BlockSpec(memory_space=pl.ANY)] * len(awaited),
        out_specs=(IN_VMEM,) * 2,
        scratch_shapes=[
            pltpu.VMEM((rows, LOCAL_WIDTH), BF16),
            pltpu.VMEM((LOCAL_WIDTH, rows), BF16),
            pltpu.VMEM((rows, LOCAL_WIDTH), BF16),
            pltpu.VMEM((LOCAL_HEADS, rows, HDIM), F32),
            pltpu.VMEM((LOCAL_HEADS, rows, HDIM), F32),
            pltpu.VMEM((LOCAL_HEADS, rows, BLOCK), F32),
            pltpu.VMEM((LOCAL_HEADS, rows, BLOCK), F32),
        ],
        compiler_params=pltpu.CompilerParams(vmem_limit_bytes=40 * 2**20),
        cost_estimate=pl.CostEstimate(flops=rows, bytes_accessed=rows, transcendentals=0),
    )(order, projected, grad_mixed, log_total, segments[None, :], segments[:, None], *awaited)


def qkv_forward(normed_all, weight_heads):
    return dot_f32("td,dc->tc", normed_all, weight_heads[:, : 3 * LOCAL_WIDTH]).astype(BF16)


def out_forward(mixed, weight_heads):
    return dot_f32("td,od->to", mixed, weight_heads[:, 3 * LOCAL_WIDTH :])


def feed_forward(normed_all, weight_up, weight_down):
    hidden = dot_f32("td,fd->tf", normed_all, weight_up)
    active = gelu_tanh(hidden).astype(BF16)
    return dot_f32("tf,fd->td", active, weight_down), hidden, active


def feed_backward(weight_up, weight_down, hidden, grad_low):
    grad_active = dot_f32("td,fd->tf", grad_low, weight_down)
    grad_hidden = jax.vjp(gelu_tanh, hidden)[1](grad_active)[0].astype(BF16)
    return grad_hidden, dot_f32("tf,fd->td", grad_hidden, weight_up)


def times(rows, gram):
    return jnp.dot(rows.astype(BF16), gram, preferred_element_type=F32)


def newton_two(rows, gram, scale):
    def polynomial(values):
        once = times(values, gram)
        return NEWTON_A * values + NEWTON_B * once + NEWTON_C * times(once, gram)

    first = polynomial(rows / scale)
    once = polynomial(times(polynomial(first), gram))
    twice = polynomial(times(polynomial(once), gram))
    return NEWTON_A * first + NEWTON_B * once + NEWTON_C * twice


def exact(left, right):
    return jnp.dot(left, right, precision=HIGHEST)


def newton_heads(block):
    gram = jnp.einsum("br,cr->bc", block, block, precision=HIGHEST)
    scale = jnp.sqrt(jnp.trace(gram)) + NEWTON_EPSILON
    gram = gram / (scale * scale)
    one = jnp.eye(HDIM, dtype=F32)
    first = NEWTON_A * one + NEWTON_B * gram + NEWTON_C * exact(gram, gram)
    gram = exact(exact(first, gram), first)
    second = NEWTON_A * one + NEWTON_B * gram + NEWTON_C * exact(gram, gram)
    return exact(exact(second, first), block / scale)


def body(
    inputs,
    cotangent,
    segment_ids,
    routed,
    qkv_master,
    out_master,
    up_master,
    down_master,
    qkv_moment,
    out_moment,
    up_moment,
    down_moment,
    router,
    router_first,
    router_second,
):
    masters = (qkv_master, out_master, up_master, down_master)
    token_count = inputs.shape[0]
    core, place_z = lax.axis_index("c"), lax.axis_index("z")
    batch_index = 2 * place_z + core
    all_tokens = jnp.arange(token_count * N_BATCH)

    at = jnp.arange(N_BATCH)
    order = (4 * ((at + core) % 2) + (at // 2 - place_z) % 4).astype(jnp.int32)
    block_of = 2 * ((at % 4 + place_z) % 4) + (at // 4 + core) % 2
    row_pos = (block_of[:, None] * token_count + jnp.arange(token_count)[None, :]).reshape(-1)
    block_of = block_of.astype(jnp.int32)
    single = jnp.zeros((1,), jnp.int32)

    normed_round = gather_near(rms_norm(inputs).astype(BF16))
    heads_local, segments_all = head_shards(masters, segment_ids)
    tied = lax.optimization_barrier((heads_local, *normed_round[1]))
    heads_local, normed_round = tied[0], (normed_round[0], tied[1:])
    heads_pair = jnp.concatenate([heads_local[1, :32], heads_local[1, 32:]], axis=1)
    wide_dense = jnp.stack([up_master[0].astype(BF16), down_master[0].astype(BF16), heads_pair])
    wide_dense = lax.all_gather(wide_dense, FSDP, axis=1, tiled=True)
    up_dense, down_dense = wide_dense[0], wide_dense[1]
    heads_pair = wide_dense[2].reshape(N_FSDP, 32, 2, 4 * LOCAL_WIDTH)
    heads_routed = jnp.transpose(heads_pair, (0, 2, 1, 3)).reshape(D, 4 * LOCAL_WIDTH)
    heads_round = gather_fsdp_first(heads_local[0])
    normed_round = gather_far(normed_round)
    tied = lax.optimization_barrier((*heads_round[1], *normed_round[1]))
    out_low = jnp.concatenate([out_master[0], out_master[1]], axis=1).astype(BF16)
    out_low = lax.all_gather(out_low, EVERY, axis=0, tiled=True)
    out_dense, out_routed = out_low[:, :D], out_low[:, D:]
    wide_routed = jnp.stack([up_master[1], down_master[1]]).astype(BF16)
    wide_routed = lax.all_gather(wide_routed, FSDP, axis=1, tiled=True)
    up_routed, down_routed = wide_routed[0], wide_routed[1]
    heads_round = gather_fsdp_second((heads_round[0], tied[:3]))
    normed_round = gather_core((normed_round[0], tied[3:]))
    heads_dense = gather_fsdp_value(heads_round)
    normed_low = gather_value(normed_round)

    chosen = routed[0]
    local_index = chosen - batch_index * token_count
    pick = (local_index[:, None] == jnp.arange(token_count)[None, :]).astype(F32)
    pick_all = (chosen[:, None] == row_pos[None, :]).astype(BF16)
    not_routed = 1.0 - jnp.max(pick, axis=0)[:, None]
    rest_grads = cotangent * not_routed
    slot_segments = jnp.sum(
        jnp.where(chosen[:, None] == all_tokens[None, :], segments_all[None, :], 0.0), axis=1
    )

    moments_heads = jnp.concatenate([qkv_moment, out_moment], axis=2).reshape(
        2, 8, 4, N_BATCH, LOCAL_WIDTH
    )
    moments_heads = jnp.transpose(moments_heads, (0, 2, 3, 1, 4))[:, :, None]
    moments_heads = jnp.broadcast_to(moments_heads, (2, 4, LOCAL_HEADS, N_BATCH, 8, LOCAL_WIDTH))
    moment_block = lax.all_to_all(
        moments_heads.reshape(128, 8, LOCAL_WIDTH), EVERY, split_axis=0, concat_axis=0, tiled=True
    ).reshape(D, LOCAL_WIDTH)
    moment_block = lax.dynamic_slice_in_dim(
        jnp.transpose(moment_block), lax.axis_index("x") % 2 * HDIM, HDIM, 0
    )

    def of_slots(values):
        return jnp.einsum("st,td->sd", pick_all, values, preferred_element_type=F32).astype(BF16)

    start_rows = dot_f32(
        "st,td->sd", pick.astype(BF16), jnp.concatenate([inputs, cotangent], axis=1).astype(BF16)
    )
    start_round = sum_near(sum_core(after(start_rows, heads_dense)))
    projected = qkv_forward(normed_low, heads_dense)
    mixed_low, mixed_line, log_total = attend(
        projected, order, segments_all, *start_round[0]
    )
    mixed_slots = of_slots(mixed_low)

    slot_round = columns_core(mixed_slots)
    start_round = sum_next(
        (start_round[0], lax.optimization_barrier(start_round[1] + (mixed_slots,))[:2])
    )
    slot_round = columns_near(slot_round)
    start_round = sum_last(
        (start_round[0], lax.optimization_barrier(start_round[1] + slot_round[0])[:2])
    )
    slot_inputs = sum_value(start_round)
    slot_inputs, slot_grads = slot_inputs[:, :D], slot_inputs[:, D:]
    slot_middle = slot_inputs + dot_f32(
        "td,od->to", columns_value(slot_round), out_dense
    )
    slot_two = rms_norm(slot_middle).astype(BF16)
    slot_fed, slot_hidden, slot_active = feed_forward(slot_two, up_dense, down_dense)

    fed_round = sum_core(slot_fed)
    mixed_round = rows_core(after(mixed_low, *fed_round[0]))
    fed_round = sum_near(fed_round)
    mixed_round = rows_near(mixed_round)
    fed_round, mixed_rows = during(fed_round, lambda late: columns_value(mixed_round, moment_block))
    fed_round = sum_next(fed_round)

    def rest_forward(late):
        middle = inputs + dot_f32("td,od->to", late(mixed_rows), out_dense)
        return middle, rms_norm(middle).astype(BF16)

    fed_round, (middle, rest_two_low) = during(fed_round, rest_forward)
    fed_round = sum_last(fed_round)
    normed_two = lax.all_gather(rest_two_low, BATCH, axis=0, tiled=True)
    rest_low = lax.all_gather(
        after(rest_grads.astype(BF16), rest_two_low), BATCH, axis=0, tiled=True
    )
    slot_rows = slot_middle + sum_value(fed_round)

    slot_normed = rms_norm(slot_rows)
    slot_low = slot_normed.astype(BF16)
    r_projected = qkv_forward(slot_low, heads_routed)
    r_mixed, _, r_log_total = attend(r_projected, single, slot_segments)
    r_round = columns_core(r_mixed)
    gate_values = jnp.dot(slot_normed, router, precision=HIGHEST)
    r_round = columns_near(r_round)
    r_attended = dot_f32("td,od->to", columns_value(r_round), out_routed)
    r_middle = slot_rows + r_attended
    r_two = rms_norm(r_middle).astype(BF16)
    r_fed_part, r_hidden, r_active = feed_forward(r_two, up_routed, down_routed)

    r_round = sum_near(sum_core(r_fed_part))

    def rest_active(late):
        _, hidden, active = feed_forward(late(normed_two), up_dense, down_dense)
        return hidden, active

    r_round, (feed_hidden, feed_active) = during(r_round, rest_active)
    r_round = sum_last(sum_next(r_round))
    routed_branch = r_attended + sum_value(r_round)

    branch_grads = gate_values[:, None] * slot_grads
    branch_low = branch_grads.astype(BF16)
    r_grad_hidden, r_grad_two = feed_backward(up_routed, down_routed, r_hidden, branch_low)

    r_round = sum_near(sum_core(r_grad_two))

    def rest_back(late):
        grad_active = dot_f32("td,fd->tf", late(rest_low), down_dense)
        return jax.vjp(gelu_tanh, feed_hidden)[1](grad_active)[0].astype(BF16)

    r_round, rest_hidden = during(r_round, rest_back)
    r_round = sum_next(r_round)
    r_round, rest_two = during(r_round, lambda late: dot_f32("tf,fd->td", late(rest_hidden), up_dense))
    rest_two = lax.psum_scatter(rest_two.astype(BF16), BATCH, scatter_dimension=0, tiled=True)
    r_round = sum_last(r_round)

    def routed_weights(late):
        return (
            dot_f32("tf,td->fd", late(r_grad_hidden), r_two),
            dot_f32("tf,td->fd", r_active, late(branch_low)),
            jnp.sum(slot_grads * routed_branch, axis=1),
        )

    r_round, (r_grad_up, r_grad_down, gate_grads) = during(r_round, routed_weights)
    r_grad_mid = norm_back(r_middle, sum_value(r_round))
    r_grad_low = (r_grad_mid + branch_grads).astype(BF16)

    def out_back(grad_low, weight_heads):
        return dot_f32("to,od->td", grad_low, weight_heads[:, 3 * LOCAL_WIDTH :]).astype(BF16)

    r_grad_projected, _ = attend_back(
        r_projected, single, slot_segments, r_log_total, out_back(r_grad_low, heads_routed)
    )
    r_round = sum_core(dot_f32("tc,dc->td", r_grad_projected, heads_routed[:, : 3 * LOCAL_WIDTH]))
    r_round = sum_near(r_round)
    r_round, rest_up = during(
        r_round, lambda late: dot_f32("tf,td->fd", late(rest_hidden), normed_two)
    )
    r_round = sum_next(r_round)
    r_round, rest_down = during(
        r_round, lambda late: dot_f32("tf,td->fd", feed_active, late(rest_low))
    )
    r_round = sum_last(r_round)
    r_grad_normed = sum_value(r_round)
    slot_out_grads = (
        slot_grads
        + r_grad_mid
        + norm_back(slot_rows, r_grad_normed + gate_grads[:, None] * router[None, :])
    )

    slot_out_low = slot_out_grads.astype(BF16)
    slot_grad_hidden, slot_grad_two = feed_backward(up_dense, down_dense, slot_hidden, slot_out_low)
    slot_round = sum_near(sum_core(slot_grad_two))
    def routed_heads(late):
        return (
            dot_f32("tc,td->cd", late(r_grad_projected), slot_low),
            dot_f32("td,to->do", r_mixed, late(r_grad_low)),
        )

    slot_round, (r_grad_qkv, r_grad_out) = during(slot_round, routed_heads)
    slot_round = sum_next(slot_round)
    slot_round, fed_line = during(
        slot_round, lambda late: dot_f32("tf,fd->td", late(feed_active), down_dense)
    )
    slot_round = sum_last(slot_round)
    slot_mid = slot_out_grads + norm_back(slot_middle, sum_value(slot_round))
    slot_mid_low = slot_mid.astype(BF16)
    slot_mixed = out_back(slot_mid_low, heads_dense)
    grad_up = rest_up + dot_f32("tf,td->fd", slot_grad_hidden, slot_two)
    grad_down = rest_down + dot_f32("tf,td->fd", slot_active, slot_out_low)
    wide_round = scatter_fsdp_first(grad_up, r_grad_up, grad_down, r_grad_down)

    rest_two = after(rest_two, *wide_round[0], slot_mixed)
    rest_mid = rest_grads + norm_back(middle, rest_two.astype(F32))
    rest_mid_low = rest_mid.astype(BF16)
    rest_mixed = dot_f32("to,od->td", rest_mid_low, out_dense).astype(BF16)
    rest_mid_all = lax.all_gather(rest_mid_low, BATCH, axis=0, tiled=True)
    rest_mixed = back_value(back_near(back_core(rest_mixed)))
    grad_mixed = (
        rest_mixed.astype(F32)
        + jnp.einsum("st,sd->td", pick_all, slot_mixed, preferred_element_type=F32)
    ).astype(BF16)
    grad_mixed = after(grad_mixed, *wide_round[0])
    fed_rows = lax.psum_scatter(after(fed_line, grad_mixed), BATCH, scatter_dimension=0, tiled=True)
    grad_projected, grad_projected_line = attend_back(projected, order, segments_all, log_total, grad_mixed)

    wide_round = (
        wide_round[0],
        lax.optimization_barrier(wide_round[1] + (grad_projected,))[:3],
    )
    wide_round = scatter_fsdp_second(wide_round)

    def dense_weights(late):
        grads = late(grad_projected)
        grad_qkv = dot_f32("tc,td->cd", grads, normed_low)
        grad_out = dot_f32("td,to->do", mixed_line, rest_mid_all) + dot_f32(
            "td,to->do", mixed_slots, slot_mid_low
        )
        return grad_qkv, grad_out

    wide_round, (grad_qkv, grad_out) = during(wide_round, dense_weights)

    block_parts = jnp.concatenate([grad_qkv, grad_out, r_grad_qkv, r_grad_out], axis=0).astype(BF16)
    router_grad = jnp.dot(gate_grads, slot_normed, precision=HIGHEST)
    router_high = router_grad.astype(BF16)
    router_low = (router_grad - router_high.astype(F32)).astype(BF16)
    router_rows = jnp.concatenate(
        [router_high[None, :], router_low[None, :], jnp.zeros((14, D), BF16)], axis=0
    )
    block_parts = jnp.concatenate(
        [block_parts.reshape(16, HDIM, D), jnp.broadcast_to(router_rows[None], (16, 16, D))], axis=1
    )
    heads_round = scatter_fsdp_first(block_parts.reshape(-1, D))

    wide_grads = turn_total(wide_round).reshape(4, 32, D)
    new_up_moment = MOMENTUM * up_moment + wide_grads[:2]
    new_down_moment = MOMENTUM * down_moment + wide_grads[2:]
    wide_own = after(jnp.concatenate([new_up_moment, new_down_moment], axis=0), *heads_round[0])
    wide_round = exchange_near(wide_own)
    wide_round, grad_normed = during(
        wide_round,
        lambda late: dot_f32("tc,dc->td", late(grad_projected_line), heads_dense[:, : 3 * LOCAL_WIDTH]),
    )
    wide_rows = exchange_value(wide_round)
    rows_low = wide_rows.astype(BF16)
    rows_both = jnp.concatenate([rows_low, shift(rows_low, "c", 1)], axis=0)
    heads_round = (heads_round[0], lax.optimization_barrier(heads_round[1] + (rows_both,))[:3])
    heads_round = turn_parts(turn_total(heads_round), True)
    rows_both = after(rows_both, *heads_round[0])
    grad_normed = lax.psum_scatter(
        after(grad_normed, rows_both), BATCH, scatter_dimension=0, tiled=True
    )
    own_columns = lax.dynamic_slice_in_dim(rows_both, core * (D // 2), D // 2, 1)
    gram_part = dot_f32("rb,rc->bc", own_columns, rows_both)

    def heads_step(late):
        grads = turn_total(heads_round)
        new_block = MOMENTUM * moment_block + late(grads)[:HDIM]
        ortho_block = newton_heads(new_block)
        returned = jnp.transpose(jnp.concatenate([new_block, ortho_block], axis=0))
        return returned.reshape(128, 8, 2 * HDIM), grads[HDIM] + grads[HDIM + 1]

    gram_round = turn_second(turn_first(gram_part))
    gram_round, (returned, router_total) = during(gram_round, heads_step)
    gram_round = turn_third(gram_round)
    returned = lax.all_to_all(returned, EVERY, split_axis=0, concat_axis=0, tiled=True)
    gram_round = turn_fourth(gram_round)
    gram_round, mixed = during(
        gram_round,
        lambda late: middle
        + late(fed_rows)
        + jnp.einsum("st,sd->td", pick, gate_values[:, None] * routed_branch, precision=HIGHEST),
    )
    gram_half = turn_value(gram_round)
    gram_other = shift(gram_half, "c", 1)
    wide_gram = jnp.concatenate(
        [jnp.where(core == 0, gram_half, gram_other), jnp.where(core == 0, gram_other, gram_half)],
        axis=0,
    )
    wide_scale = jnp.sqrt(jnp.trace(wide_gram.astype(F32))) + NEWTON_EPSILON
    wide_gram = (wide_gram.astype(F32) / (wide_scale * wide_scale)).astype(BF16)
    wide_ortho = newton_two(wide_rows, wide_gram, wide_scale).reshape(4, 32, D)
    wide_round = exchange_near(wide_ortho)

    def token_step(late):
        grad_mid = rest_mid + jnp.einsum("st,sd->td", pick, slot_mid, precision=HIGHEST)
        grad_inputs = grad_mid + norm_back(inputs, late(grad_normed))
        return grad_inputs

    wide_round, grad_inputs = during(wide_round, token_step)
    wide_ortho = exchange_value(wide_round).reshape(4, 32, D)

    returned = returned.reshape(2, 4, LOCAL_HEADS, N_BATCH, 8, 2, HDIM)
    returned = jnp.transpose(returned, (5, 0, 4, 1, 3, 2, 6)).reshape(2, 2, 8, 4 * D)
    new_moments = (returned[0, :, :, : 3 * D], returned[0, :, :, 3 * D :], new_up_moment, new_down_moment)
    orthos = (returned[1, :, :, : 3 * D], returned[1, :, :, 3 * D :], wide_ortho[:2], wide_ortho[2:])

    widths = (HDIM, HDIM, D, D)
    full_rows = (D, D, FF, FF)
    new_masters = []
    for index_type in range(4):
        rate = STEP_RATES[index_type]
        factor = 0.2 * math.sqrt(max(full_rows[index_type], widths[index_type]))
        new_masters.append(
            masters[index_type] * (1.0 - rate * WEIGHT_DECAY) - rate * factor * orthos[index_type]
        )
    first_new = FIRST_DECAY * router_first + (1.0 - FIRST_DECAY) * router_total
    second_new = SECOND_DECAY * router_second + (1.0 - SECOND_DECAY) * router_total * router_total
    corrected_first = first_new / (1.0 - FIRST_DECAY**STEP)
    corrected_second = second_new / (1.0 - SECOND_DECAY**STEP)
    router_new = router * (1.0 - ADAM_RATE * WEIGHT_DECAY) - ADAM_RATE * corrected_first / (
        jnp.sqrt(corrected_second) + ADAM_EPSILON
    )
    return (
        (mixed, grad_inputs)
        + new_moments
        + tuple(new_masters)
        + tuple(master.astype(BF16) for master in new_masters)
        + (router_new, first_new, second_new)
    )


def solution(mesh):
    fine = Mesh(mesh.devices.reshape(4, 4, 4, 2), EVERY)
    tokens = P(EVERY, None)
    weights = P(None, EVERY, None)
    return jax.shard_map(
        body,
        mesh=fine,
        in_specs=(tokens, tokens, P(EVERY), P(FSDP, None)) + (weights,) * 8 + (P(),) * 3,
        out_specs=(tokens, tokens) + (weights,) * 12 + (P(),) * 3,
        check_vma=False,
    )
```
